128 devices in a mesh: dp: 16 (over x, z), tensor: 8 (over y, core).
Axes of the slice: x: 4, y: 4, z: 4, core: 2. Of those that a mesh axis runs over, the one named last changes fastest.
Arguments:
- tokens: bfloat16 [8192, 8192], P('dp', 'tensor'), may hold values from -120 to 120
- block_target: int32 [64], P('dp'), may hold values from 0 to 63, as said below
- doc_lengths: int32 [16, 6], P('dp'), may hold values from 1 to 256, 512 in all within a row
- qkv_weight: bfloat16 [8192, 10240], P(None, 'tensor'), may hold values from -0.0625 to 0.0625
- out_grad: bfloat16 [8192, 8192], P('dp', 'tensor'), may hold values from -6 to 6
Outputs:
- attn_out: bfloat16 [8192, 8192], P('dp', 'tensor')
- weight_grad: float32 [8192, 10240], P('dp', 'tensor')
The draws below stay inside these ranges and needn't reach their ends.
Inputs may be any that keep to these rules, and one draw needn't show every extreme that they name: `block_target`: A permutation of the block positions: entry b is the position after the move of block b, as device * 4 + slot. The 4 blocks of one device go to as many different devices, at most one block to each, and every device receives exactly 4 blocks.
All inputs are finite; a program needn't handle non-finite values.
Results may differ from the reference program's by a relative error of at most 0.02.
Values may be sent and summed in bfloat16 or wider, within the bound.
A program may use at most 192 MiB of HBM per device.

```python
import math
import jax
import jax.numpy as jnp
import numpy as np
from jax import lax

D = 8192
HD = 128
QH = 64
KVH = 8
GQ = 8
COLS = 10240
BLK = 128
TOK_DEV = 512
DOCS = 6
TOKENS = 8192
N_DP = 16


def draw_tokens(key, part):
    key = jax.random.fold_in(key, 11)
    key_noise, key_pair = jax.random.split(key, 2)
    base = jax.random.truncated_normal(key_noise, -5.0, 5.0, (TOKENS, D), jnp.float32)
    row_groups = TOKENS // TOK_DEV
    pairing = jax.random.permutation(key_pair, row_groups)
    row_group = jnp.arange(TOKENS) // TOK_DEV
    col_group = jnp.arange(D) // (D // row_groups)
    spike = jnp.where(pairing[row_group][:, None] == col_group[None, :], 3.0, 1.0)
    return (base * spike).astype(jnp.bfloat16)


def draw_block_target(key, part):
    key = jax.random.fold_in(key, 5)
    key_offset, key_in, key_out, key_order, key_slot = jax.random.split(key, 5)
    peer_count = TOKENS // TOK_DEV
    block_count = TOK_DEV // BLK
    offsets = jax.random.permutation(key_offset, peer_count)[:block_count]
    label_in = jax.random.permutation(key_in, peer_count)
    label_out = jax.random.permutation(key_out, peer_count)
    order_keys = jax.random.split(key_order, peer_count)
    slot_keys = jax.random.split(key_slot, peer_count)
    group_of = jax.vmap(lambda item: jax.random.permutation(item, block_count))(order_keys)
    slot_of = jax.vmap(lambda item: jax.random.permutation(item, block_count))(slot_keys)
    source = jnp.arange(peer_count)[:, None]
    target_dev = label_out[(label_in[source] + offsets[group_of]) % peer_count]
    target_slot = slot_of[target_dev, group_of]
    return (target_dev * block_count + target_slot).reshape(-1).astype(jnp.int32)


def block_levels(own_key, shape, shards, low, top_value):
    factor_of, own = 1.0, jax.random.fold_in(own_key, 6)
    for axis_at, shards_of in shards:
        heights = jnp.exp(jax.random.uniform(jax.random.fold_in(own, axis_at), (shards_of,), jnp.float32, low / len(shards), top_value / len(shards)))
        factor_of = factor_of * jnp.repeat(heights, shape[axis_at] // shards_of).reshape([-1 if axis == axis_at else 1 for axis in range(len(shape))])
    return factor_of


def split_up(count, total, bound, skew):
    weights = [(1 << 20) // math.isqrt(rank ** skew) + 1 for rank in range(2, count + 1)]
    rest, given = total - bound - (count - 1), [1] * (count - 1)
    while rest > 0:
        movable = [i for i in range(count - 1) if given[i] < bound]
        whole, remaining = sum([weights[i] for i in movable]), rest
        for i in movable:
            more = min(bound - given[i], max(1, remaining * weights[i] // whole), rest)
            given[i] = given[i] + more
            rest = rest - more
    return np.array([bound] + given)


def ragged_sizes(stream_key, number_of, total, reach, skew):
    if number_of == 2:
        one = jax.random.randint(stream_key, (), max(1, total - reach), min(reach, total - 1) + 1)
        return jnp.stack([one, total - one])
    tallies = jnp.asarray(split_up(number_of, total, reach, skew), jnp.int32)
    pairs = (number_of - 1) // 2
    source_of, receiver = tallies[1:1 + 2 * pairs:2], tallies[2:2 + 2 * pairs:2]
    margin = jnp.minimum(source_of - 1, reach - receiver)
    shifted = jax.random.randint(jax.random.fold_in(stream_key, 1), (pairs,), 0, 1 << 20) % (margin + 1)
    tallies = tallies.at[1:1 + 2 * pairs:2].set(source_of - shifted).at[2:2 + 2 * pairs:2].set(receiver + shifted)
    return tallies[jax.random.permutation(jax.random.fold_in(stream_key, 2), number_of)]


def noise(own_key, shape, width, reach, cuts=(), held_as=jnp.bfloat16):
    drawn = jax.random.normal(own_key, shape, jnp.float32) * width
    if len(cuts) > 0:
        drawn = block_levels(own_key, shape, cuts, -0.22, 0.18) * drawn
    return jnp.clip(drawn, min=-reach, max=reach).astype(held_as)


def setup_inputs(seed: int = 0) -> dict:
    key_of = jax.random.split(jax.random.key(seed), 6)
    tokens = draw_tokens(jax.random.fold_in(key_of[5], 71), 0)
    block_target = draw_block_target(jax.random.fold_in(key_of[5], 71), 0)
    doc_lengths = jax.vmap(lambda own: ragged_sizes(own, DOCS, TOK_DEV, TOK_DEV // 2, 2))(jax.random.split(key_of[2], N_DP)).reshape((N_DP, DOCS)).astype(jnp.int32)
    qkv_weight = noise(key_of[3], (D, COLS), D ** -0.5, 0.0625, ((1, 8),))
    out_grad = noise(key_of[4], (TOKENS, QH * HD), 1.0, 6.0, ((0, 16), (1, 8)))
    return {"tokens": tokens, "block_target": block_target, "doc_lengths": doc_lengths, "qkv_weight": qkv_weight, "out_grad": out_grad}


def head_pass(queries, key_head, value_head, grad_out, allowed, factor):
    scores = jnp.dot(queries, key_head.T, preferred_element_type=jnp.float32) * factor
    scores = jnp.where(allowed, scores, -jnp.inf)
    row_max = jnp.max(scores, axis=1, keepdims=True)
    exponent = jnp.exp(scores - row_max)
    prob_full = exponent / jnp.sum(exponent, axis=1, keepdims=True)
    prob_low = prob_full.astype(jnp.bfloat16)
    output = jnp.dot(prob_low, value_head, preferred_element_type=jnp.float32).astype(jnp.bfloat16)
    grad_prob = jnp.dot(grad_out, value_head.T, preferred_element_type=jnp.float32)
    row_dot = jnp.sum(prob_full * grad_prob, axis=1, keepdims=True)
    grad_score = (prob_full * (grad_prob - row_dot)).astype(jnp.bfloat16)
    grad_query = jnp.dot(grad_score, key_head, preferred_element_type=jnp.float32) * factor
    grad_key = jnp.dot(grad_score.T, queries, preferred_element_type=jnp.float32) * factor
    grad_value = jnp.dot(prob_low.T, grad_out, preferred_element_type=jnp.float32)
    return output, grad_query, grad_key, grad_value


def row_pass(moved_row, lengths_row, qkv_weight, grad_row):
    qkv = jnp.dot(moved_row, qkv_weight, preferred_element_type=jnp.float32).astype(jnp.bfloat16)
    doc_ends = jnp.cumsum(lengths_row)
    position = jnp.arange(TOK_DEV, dtype=jnp.int32)
    segment = jnp.sum((position[:, None] >= doc_ends[None, :]).astype(jnp.int32), axis=1)
    allowed = (segment[:, None] == segment[None, :]) & (position[None, :] <= position[:, None])
    factor = HD ** -0.5
    group_width = (GQ + 2) * HD
    outputs = []
    grad_columns = []
    for group_idx in range(KVH):
        base_col = group_idx * group_width
        key_head = qkv[:, base_col + GQ * HD:base_col + (GQ + 1) * HD]
        value_head = qkv[:, base_col + (GQ + 1) * HD:base_col + (GQ + 2) * HD]
        key_grad = jnp.zeros((TOK_DEV, HD), jnp.float32)
        value_grad = jnp.zeros((TOK_DEV, HD), jnp.float32)
        for head_idx in range(GQ):
            column = base_col + head_idx * HD
            out_col = (group_idx * GQ + head_idx) * HD
            output, grad_query, grad_key, grad_value = head_pass(
                qkv[:, column:column + HD], key_head, value_head,
                grad_row[:, out_col:out_col + HD], allowed, factor)
            outputs.append(output)
            grad_columns.append(grad_query.astype(jnp.bfloat16))
            key_grad = key_grad + grad_key
            value_grad = value_grad + grad_value
        grad_columns.append(key_grad.astype(jnp.bfloat16))
        grad_columns.append(value_grad.astype(jnp.bfloat16))
    grad_qkv = jnp.concatenate(grad_columns, axis=1)
    term = lax.dot_general(moved_row, grad_qkv, (((0,), (0,)), ((), ())), preferred_element_type=jnp.float32)
    return jnp.concatenate(outputs, axis=1), term.astype(jnp.bfloat16)


def reference(tokens, block_target, doc_lengths, qkv_weight, out_grad):
    block_total = TOKENS // BLK
    blocks = tokens.reshape(block_total, BLK, D)
    moved = jnp.zeros_like(blocks).at[block_target.astype(jnp.int32)].set(blocks)
    moved = moved.reshape(TOKENS // TOK_DEV, TOK_DEV, D)
    grads = out_grad.reshape(TOKENS // TOK_DEV, TOK_DEV, QH * HD)

    def step_row(total, pieces):
        moved_row, lengths_row, grad_row = pieces
        output, term = row_pass(moved_row, lengths_row, qkv_weight, grad_row)
        return total + term.astype(jnp.float32), output

    start_total = jnp.zeros((D, COLS), jnp.float32)
    weight_grad, outputs = lax.scan(step_row, start_total, (moved, doc_lengths, grads))
    return outputs.reshape(TOKENS, QH * HD), weight_grad
```

```python
import functools

import jax
import jax.numpy as jnp
from jax import lax
from jax.experimental import pallas as pl
from jax.experimental.pallas import tpu as pltpu
from jax.sharding import PartitionSpec as P

HD = 128
GQ = 8
BLK = 128
RING = 4
CHUNK = 256
MESH = pl.DeviceIdType.MESH


def head_pass(queries, key_head, value_head, grad_out, allowed, factor):
    scores = jnp.dot(queries, key_head.T, preferred_element_type=jnp.float32) * factor
    scores = jnp.where(allowed, scores, -jnp.inf)
    row_max = jnp.max(scores, axis=1, keepdims=True)
    exponent = jnp.exp(scores - row_max)
    prob_full = exponent / jnp.sum(exponent, axis=1, keepdims=True)
    prob_low = prob_full.astype(jnp.bfloat16)
    output = jnp.dot(prob_low, value_head, preferred_element_type=jnp.float32).astype(jnp.bfloat16)
    grad_prob = jnp.dot(grad_out, value_head.T, preferred_element_type=jnp.float32)
    row_dot = jnp.sum(prob_full * grad_prob, axis=1, keepdims=True)
    grad_score = (prob_full * (grad_prob - row_dot)).astype(jnp.bfloat16)
    grad_query = jnp.dot(grad_score, key_head, preferred_element_type=jnp.float32) * factor
    grad_key = jnp.dot(grad_score.T, queries, preferred_element_type=jnp.float32) * factor
    grad_value = jnp.dot(prob_low.T, grad_out, preferred_element_type=jnp.float32)
    return (output, grad_query, grad_key, grad_value)


def weight_term(gathered, grad_block):
    return lax.dot_general(
        gathered, grad_block, (((0,), (0,)), ((), ())), preferred_element_type=jnp.float32
    )


def peer_at(me, step):
    along_x = (me // RING + step // RING) % RING
    along_z = (me % RING + step % RING) % RING
    return along_x * RING + along_z


def forward_kernel(
    target_ref, tok_ref, w_ref, qkv_ref, g_out_ref,
    tag_out, tags, tags_smem, out_buf, arr0, arr1, arr2, arr3, g, w_buf, acc,
    tag_send, tag_recv, move_send, move_recv, y_send, y_recv, w_sem, smem_sem, g_sem,
):
    arrived = (arr0, arr1, arr2, arr3)
    parts = len(arrived)
    blocks = tok_ref.shape[0]
    peers = out_buf.shape[1]
    rows = blocks * BLK
    me = lax.axis_index("dp")
    tens = lax.axis_index("tensor")
    along_y, core = tens // 2, tens % 2
    up = ((along_y + 1) % RING) * 2 + core
    down = ((along_y + RING - 1) % RING) * 2 + core
    far = ((along_y + 2) % RING) * 2 + core
    twin = along_y * 2 + 1 - core

    def weight_copy(part):
        return pltpu.make_async_copy(w_ref.at[:, part], w_buf.at[part], w_sem.at[part])

    for part in range(parts):
        weight_copy(part).start()

    row_of = lax.broadcasted_iota(jnp.int32, tag_out.shape, 0)
    tile = jnp.zeros(tag_out.shape, jnp.int32)
    for slot in range(blocks):
        tile = jnp.where(row_of == slot, target_ref[slot], tile)
    tag_out[...] = tile

    def block_for(peer):
        picked = jnp.int32(0)
        for slot in range(blocks):
            picked = jnp.where(target_ref[slot] // blocks == peer, slot, picked)
        return picked

    def pack(part):
        @pl.loop(0, peers)
        def _(peer):
            out_buf[part, peer] = tok_ref[block_for(peer), :, part * CHUNK : (part + 1) * CHUNK]

    barrier = pltpu.get_barrier_semaphore()

    @pl.loop(1, peers)
    def _(step):
        pl.semaphore_signal(barrier, inc=1, device_id=(peer_at(me, step), tens), device_id_type=MESH)

    for other in (up, down, twin):
        pl.semaphore_signal(barrier, inc=1, device_id=(me, other), device_id_type=MESH)
    pack(0)
    pl.semaphore_wait(barrier, peers - 1 + 3)

    def tag_copy(step):
        return pltpu.make_async_remote_copy(
            src_ref=tag_out, dst_ref=tags.at[me],
            send_sem=tag_send.at[step], recv_sem=tag_recv.at[step],
            device_id=(peer_at(me, step), tens), device_id_type=MESH,
        )

    def move_copy(part, step):
        peer = peer_at(me, step)
        return pltpu.make_async_remote_copy(
            src_ref=out_buf.at[part, peer], dst_ref=arrived[part].at[me],
            send_sem=move_send.at[part, step], recv_sem=move_recv.at[part, step],
            device_id=(peer, tens), device_id_type=MESH,
        )

    @pl.loop(1, peers)
    def _(step):
        tag_copy(step).start()

    def send_part(part):
        @pl.loop(1, peers)
        def _(step):
            move_copy(part, step).start()

        arrived[part][me] = out_buf[part, me]

    send_part(0)
    for part in range(1, parts):
        pack(part)
        send_part(part)
    tags[me] = tag_out[...]

    @pl.loop(1, peers)
    def _(step):
        tag_copy(step).wait()

    to_smem = pltpu.make_async_copy(tags, tags_smem, smem_sem)
    to_smem.start()
    to_smem.wait()

    def source_of(slot):
        def look(peer, found):
            for entry in range(blocks):
                found = jnp.where(tags_smem[peer, entry, 0] == me * blocks + slot, peer, found)
            return found

        return lax.fori_loop(0, peers, look, jnp.int32(0))

    sources = [source_of(slot) for slot in range(blocks)]

    def lanes(which):
        return pl.ds(pl.multiple_of(which * CHUNK, CHUNK), CHUNK)

    def gather_copy(part, kind, owner, dest, first, count):
        piece = g.at[part, pl.ds(first, count), lanes(owner)]
        return pltpu.make_async_remote_copy(
            src_ref=piece, dst_ref=piece,
            send_sem=y_send.at[part, kind], recv_sem=y_recv.at[part, kind],
            device_id=(me, dest), device_id_type=MESH,
        )

    half = rows // 2

    routes = (
        (tens, up, 0, rows),
        (tens, down, 0, rows),
        (tens, twin, 0, rows),
        (down, up, 0, half),
        (down, twin, 0, rows),
        (up, down, half, half),
        (up, twin, 0, rows),
        (far, twin, 0, rows),
    )

    def hop(part, kind):
        owner, dest, first, count = routes[kind]
        return gather_copy(part, kind, owner, dest, first, count)

    def multiply(part):
        for kind in (2, 4, 6, 7):
            hop(part, kind).wait_recv()
        weight_copy(part).wait()
        out = pltpu.make_async_copy(g.at[part], g_out_ref.at[part], g_sem.at[part])
        out.start()

        @pl.loop(0, acc.shape[1] // CHUNK)
        def _(column):
            at = lanes(column)
            weights = w_buf[part, :, :, at].reshape(g.shape[2], CHUNK)
            term = jnp.dot(g[part], weights, preferred_element_type=jnp.float32)
            if part == 0:
                acc[:, at] = term
            elif part < parts - 1:
                acc[:, at] += term
            else:
                qkv_ref[:, at] = (acc[:, at] + term).astype(qkv_ref.dtype)

    for part in range(parts):
        @pl.loop(1, peers)
        def _(step):
            move_copy(part, step).wait_recv()

        for slot in range(blocks):
            g[part, slot * BLK : (slot + 1) * BLK, lanes(tens)] = arrived[part][sources[slot]]
        for kind in (0, 1, 2):
            hop(part, kind).start()
        if part > 0:
            multiply(part - 1)
        hop(part, 0).wait_recv()
        hop(part, 3).start()
        hop(part, 4).start()
        hop(part, 1).wait_recv()
        hop(part, 5).start()
        hop(part, 6).start()
        hop(part, 3).wait_recv()
        hop(part, 5).wait_recv()
        hop(part, 7).start()
    multiply(parts - 1)

    for part in range(parts):
        for kind in range(len(routes)):
            hop(part, kind).wait_send()

        @pl.loop(1, peers)
        def _(step):
            move_copy(part, step).wait_send()

        pltpu.make_async_copy(g.at[part], g_out_ref.at[part], g_sem.at[part]).wait()


def forward_call(block_target, tokens, qkv_weight, peers):
    tok_dev, width = tokens.shape
    blocks = tok_dev // BLK
    parts = width // CHUNK
    depth, columns = qkv_weight.shape
    tensors = depth // width
    deep = depth // parts
    return pl.pallas_call(
        forward_kernel,
        out_shape=(
            jax.ShapeDtypeStruct((tok_dev, columns), jnp.bfloat16),
            jax.ShapeDtypeStruct((parts, tok_dev, deep), jnp.bfloat16),
        ),
        in_specs=[
            pl.BlockSpec(memory_space=pltpu.SMEM),
            pl.BlockSpec(memory_space=pltpu.VMEM),
            pl.BlockSpec(memory_space=pl.ANY),
        ],
        out_specs=(pl.BlockSpec(memory_space=pltpu.VMEM), pl.BlockSpec(memory_space=pl.ANY)),
        scratch_shapes=[
            pltpu.VMEM((8, 128), jnp.int32),
            pltpu.VMEM((peers, 8, 128), jnp.int32),
            pltpu.SMEM((peers, 8, 128), jnp.int32),
            pltpu.VMEM((parts, peers, BLK, CHUNK), jnp.bfloat16),
            *[pltpu.VMEM((peers, BLK, CHUNK), jnp.bfloat16) for _ in range(parts)],
            pltpu.VMEM((parts, tok_dev, deep), jnp.bfloat16),
            pltpu.VMEM((parts, tensors, CHUNK, columns), jnp.bfloat16),
            pltpu.VMEM((tok_dev, columns), jnp.float32),
            pltpu.SemaphoreType.DMA((peers,)),
            pltpu.SemaphoreType.DMA((peers,)),
            pltpu.SemaphoreType.DMA((parts, peers)),
            pltpu.SemaphoreType.DMA((parts, peers)),
            pltpu.SemaphoreType.DMA((parts, 8)),
            pltpu.SemaphoreType.DMA((parts, 8)),
            pltpu.SemaphoreType.DMA((parts,)),
            pltpu.SemaphoreType.DMA,
            pltpu.SemaphoreType.DMA((parts,)),
        ],
        compiler_params=pltpu.CompilerParams(
            collective_id=0, has_side_effects=True, vmem_limit_bytes=56 * 2**20
        ),
        cost_estimate=pl.CostEstimate(
            flops=2 * tok_dev * depth * columns, bytes_accessed=40 * 2**20, transcendentals=0
        ),
    )(
        block_target,
        tokens.reshape(blocks, BLK, width),
        qkv_weight.reshape(tensors, parts, CHUNK, columns),
    )


def local(tokens, block_target, doc_lengths, qkv_weight, out_grad):
    tok_dev, width_local = tokens.shape
    qkv, pieces = forward_call(block_target, tokens, qkv_weight, lax.axis_size("dp"))
    parts = pieces.shape[0]
    gathered = (
        pieces.reshape(parts, tok_dev, -1, CHUNK).transpose(1, 2, 0, 3).reshape(tok_dev, -1)
    )
    doc_ends = jnp.cumsum(doc_lengths[0])
    position = jnp.arange(tok_dev, dtype=jnp.int32)
    segment = jnp.sum((position[:, None] >= doc_ends[None, :]).astype(jnp.int32), axis=1)
    allowed = (segment[:, None] == segment[None, :]) & (position[None, :] <= position[:, None])
    factor = HD ** (-0.5)
    outputs = []
    grad_columns = []
    key_head = qkv[:, GQ * HD : (GQ + 1) * HD]
    value_head = qkv[:, (GQ + 1) * HD : (GQ + 2) * HD]
    key_grad = jnp.zeros((tok_dev, HD), jnp.float32)
    value_grad = jnp.zeros((tok_dev, HD), jnp.float32)
    for head_idx in range(GQ):
        column = head_idx * HD
        out_col = head_idx * HD
        output, grad_query, grad_key, grad_value = head_pass(
            qkv[:, column : column + HD],
            key_head,
            value_head,
            out_grad[:, out_col : out_col + HD],
            allowed,
            factor,
        )
        outputs.append(output)
        query_low = grad_query.astype(jnp.bfloat16)
        grad_columns.append(query_low)
        key_grad = key_grad + grad_key
        value_grad = value_grad + grad_value
    pair_low = jnp.concatenate(
        [key_grad.astype(jnp.bfloat16), value_grad.astype(jnp.bfloat16)], axis=1
    )
    grad_columns.append(pair_low)
    attn_out = jnp.concatenate(outputs, axis=1)
    grad_qkv = jnp.concatenate(grad_columns, axis=1)
    weight_grad = lax.psum_scatter(
        weight_term(gathered, grad_qkv).astype(jnp.bfloat16), "dp", scatter_dimension=0, tiled=True
    ).astype(jnp.float32)
    return (attn_out, weight_grad)


def solution(mesh):
    placed = (P("dp", "tensor"), P("dp"), P("dp", None), P(None, "tensor"), P("dp", "tensor"))
    return jax.shard_map(
        local,
        mesh=mesh,
        in_specs=placed,
        out_specs=(P("dp", "tensor"), P("dp", "tensor")),
        check_vma=False,
    )
```

```python
import functools

import jax
import jax.numpy as jnp
from jax import lax
from jax.experimental import pallas as pl
from jax.experimental.pallas import tpu as pltpu
from jax.sharding import PartitionSpec as P

HD = 128
GQ = 8
BLK = 128
RING = 4
CHUNK = 256
MESH = pl.DeviceIdType.MESH


def peer_at(me, step):
    along_x = (me // RING + step // RING) % RING
    along_z = (me % RING + step % RING) % RING
    return along_x * RING + along_z


def forward_kernel(
    target_ref, tok_ref, w_ref, qkv_ref, g_out_ref,
    tag_out, tags, tags_smem, out_buf, arr0, arr1, arr2, arr3, g, w_buf, acc,
    tag_send, tag_recv, move_send, move_recv, y_send, y_recv, w_sem, smem_sem, g_sem,
):
    arrived = (arr0, arr1, arr2, arr3)
    parts = len(arrived)
    blocks = tok_ref.shape[0]
    peers = out_buf.shape[1]
    rows = blocks * BLK
    me = lax.axis_index("dp")
    tens = lax.axis_index("tensor")
    along_y, core = tens // 2, tens % 2
    up = ((along_y + 1) % RING) * 2 + core
    down = ((along_y + RING - 1) % RING) * 2 + core
    far = ((along_y + 2) % RING) * 2 + core
    twin = along_y * 2 + 1 - core

    def weight_copy(part):
        return pltpu.make_async_copy(w_ref.at[:, part], w_buf.at[part], w_sem.at[part])

    for part in range(parts):
        weight_copy(part).start()

    row_of = lax.broadcasted_iota(jnp.int32, tag_out.shape, 0)
    tile = jnp.zeros(tag_out.shape, jnp.int32)
    for slot in range(blocks):
        tile = jnp.where(row_of == slot, target_ref[slot], tile)
    tag_out[...] = tile

    def block_for(peer):
        picked = jnp.int32(0)
        for slot in range(blocks):
            picked = jnp.where(target_ref[slot] // blocks == peer, slot, picked)
        return picked

    def pack(part):
        @pl.loop(0, peers)
        def _(peer):
            out_buf[part, peer] = tok_ref[block_for(peer), :, part * CHUNK : (part + 1) * CHUNK]

    barrier = pltpu.get_barrier_semaphore()

    @pl.loop(1, peers)
    def _(step):
        pl.semaphore_signal(barrier, inc=1, device_id=(peer_at(me, step), tens), device_id_type=MESH)

    for other in (up, down, twin):
        pl.semaphore_signal(barrier, inc=1, device_id=(me, other), device_id_type=MESH)
    pack(0)
    pl.semaphore_wait(barrier, peers - 1 + 3)

    def tag_copy(step):
        return pltpu.make_async_remote_copy(
            src_ref=tag_out, dst_ref=tags.at[me],
            send_sem=tag_send.at[step], recv_sem=tag_recv.at[step],
            device_id=(peer_at(me, step), tens), device_id_type=MESH,
        )

    def move_copy(part, step):
        peer = peer_at(me, step)
        return pltpu.make_async_remote_copy(
            src_ref=out_buf.at[part, peer], dst_ref=arrived[part].at[me],
            send_sem=move_send.at[part, step], recv_sem=move_recv.at[part, step],
            device_id=(peer, tens), device_id_type=MESH,
        )

    @pl.loop(1, peers)
    def _(step):
        tag_copy(step).start()

    def send_part(part):
        @pl.loop(1, peers)
        def _(step):
            move_copy(part, step).start()

        arrived[part][me] = out_buf[part, me]

    send_part(0)
    for part in range(1, parts):
        pack(part)
        send_part(part)
    tags[me] = tag_out[...]

    @pl.loop(1, peers)
    def _(step):
        tag_copy(step).wait()

    to_smem = pltpu.make_async_copy(tags, tags_smem, smem_sem)
    to_smem.start()
    to_smem.wait()

    def source_of(slot):
        def look(peer, found):
            for entry in range(blocks):
                found = jnp.where(tags_smem[peer, entry, 0] == me * blocks + slot, peer, found)
            return found

        return lax.fori_loop(0, peers, look, jnp.int32(0))

    sources = [source_of(slot) for slot in range(blocks)]

    def lanes(which):
        return pl.ds(pl.multiple_of(which * CHUNK, CHUNK), CHUNK)

    def gather_copy(part, kind, owner, dest, first, count):
        piece = g.at[part, pl.ds(first, count), lanes(owner)]
        return pltpu.make_async_remote_copy(
            src_ref=piece, dst_ref=piece,
            send_sem=y_send.at[part, kind], recv_sem=y_recv.at[part, kind],
            device_id=(me, dest), device_id_type=MESH,
        )

    half = rows // 2

    routes = (
        (tens, up, 0, rows),
        (tens, down, 0, rows),
        (tens, twin, 0, rows),
        (down, up, 0, half),
        (down, twin, 0, rows),
        (up, down, half, half),
        (up, twin, 0, rows),
        (far, twin, 0, rows),
    )

    def hop(part, kind):
        owner, dest, first, count = routes[kind]
        return gather_copy(part, kind, owner, dest, first, count)

    def multiply(part):
        for kind in (2, 4, 6, 7):
            hop(part, kind).wait_recv()
        weight_copy(part).wait()
        out = pltpu.make_async_copy(g.at[part], g_out_ref.at[part], g_sem.at[part])
        out.start()

        @pl.loop(0, acc.shape[1] // CHUNK)
        def _(column):
            at = lanes(column)
            weights = w_buf[part, :, :, at].reshape(g.shape[2], CHUNK)
            term = jnp.dot(g[part], weights, preferred_element_type=jnp.float32)
            if part == 0:
                acc[:, at] = term
            elif part < parts - 1:
                acc[:, at] += term
            else:
                qkv_ref[:, at] = (acc[:, at] + term).astype(qkv_ref.dtype)

    for part in range(parts):
        @pl.loop(1, peers)
        def _(step):
            move_copy(part, step).wait_recv()

        for slot in range(blocks):
            g[part, slot * BLK : (slot + 1) * BLK, lanes(tens)] = arrived[part][sources[slot]]
        for kind in (0, 1, 2):
            hop(part, kind).start()
        if part > 0:
            multiply(part - 1)
        hop(part, 0).wait_recv()
        hop(part, 3).start()
        hop(part, 4).start()
        hop(part, 1).wait_recv()
        hop(part, 5).start()
        hop(part, 6).start()
        hop(part, 3).wait_recv()
        hop(part, 5).wait_recv()
        hop(part, 7).start()
    multiply(parts - 1)

    for part in range(parts):
        for kind in range(len(routes)):
            hop(part, kind).wait_send()

        @pl.loop(1, peers)
        def _(step):
            move_copy(part, step).wait_send()

        pltpu.make_async_copy(g.at[part], g_out_ref.at[part], g_sem.at[part]).wait()


def forward_call(block_target, tokens, qkv_weight, peers):
    tok_dev, width = tokens.shape
    blocks = tok_dev // BLK
    parts = width // CHUNK
    depth, columns = qkv_weight.shape
    tensors = depth // width
    deep = depth // parts
    return pl.pallas_call(
        forward_kernel,
        out_shape=(
            jax.ShapeDtypeStruct((tok_dev, columns), jnp.bfloat16),
            jax.ShapeDtypeStruct((parts, tok_dev, deep), jnp.bfloat16),
        ),
        in_specs=[
            pl.BlockSpec(memory_space=pltpu.SMEM),
            pl.BlockSpec(memory_space=pltpu.VMEM),
            pl.BlockSpec(memory_space=pl.ANY),
        ],
        out_specs=(pl.BlockSpec(memory_space=pltpu.VMEM), pl.BlockSpec(memory_space=pl.ANY)),
        scratch_shapes=[
            pltpu.VMEM((8, 128), jnp.int32),
            pltpu.VMEM((peers, 8, 128), jnp.int32),
            pltpu.SMEM((peers, 8, 128), jnp.int32),
            pltpu.VMEM((parts, peers, BLK, CHUNK), jnp.bfloat16),
            *[pltpu.VMEM((peers, BLK, CHUNK), jnp.bfloat16) for _ in range(parts)],
            pltpu.VMEM((parts, tok_dev, deep), jnp.bfloat16),
            pltpu.VMEM((parts, tensors, CHUNK, columns), jnp.bfloat16),
            pltpu.VMEM((tok_dev, columns), jnp.float32),
            pltpu.SemaphoreType.DMA((peers,)),
            pltpu.SemaphoreType.DMA((peers,)),
            pltpu.SemaphoreType.DMA((parts, peers)),
            pltpu.SemaphoreType.DMA((parts, peers)),
            pltpu.SemaphoreType.DMA((parts, 8)),
            pltpu.SemaphoreType.DMA((parts, 8)),
            pltpu.SemaphoreType.DMA((parts,)),
            pltpu.SemaphoreType.DMA,
            pltpu.SemaphoreType.DMA((parts,)),
        ],
        compiler_params=pltpu.CompilerParams(
            collective_id=0, has_side_effects=True, vmem_limit_bytes=56 * 2**20
        ),
        cost_estimate=pl.CostEstimate(
            flops=2 * tok_dev * depth * columns, bytes_accessed=40 * 2**20, transcendentals=0
        ),
    )(
        block_target,
        tokens.reshape(blocks, BLK, width),
        qkv_weight.reshape(tensors, parts, CHUNK, columns),
    )


def backward_kernel(
    qkv_ref, grad_ref, seg_q_ref, seg_k_ref, g_ref, attn_ref, weight_grad_ref,
    mt, mt_t, grads, sums, arrived, bias, key_grad, value_grad,
    own_sem, cross_send, cross_recv, y_send, y_recv, grad_send, grad_recv, sum_send, sum_recv,
):
    rows = qkv_ref.shape[0]
    half = rows // 2
    me = lax.axis_index("dp")
    tens = lax.axis_index("tensor")
    at_x, at_z = me // RING, me % RING
    along_y, core = tens // 2, tens % 2
    up = ((along_y + 1) % RING) * 2 + core
    down = ((along_y + RING - 1) % RING) * 2 + core
    far = ((along_y + 2) % RING) * 2 + core
    twin = along_y * 2 + 1 - core
    near_x = at_x + 1 - 2 * (at_x % 2)
    near_z = at_z + 1 - 2 * (at_z % 2)
    mates = (me, near_x * RING + at_z, at_x * RING + near_z, near_x * RING + near_z)

    def mirror(device, which):
        along_x, along_z = device // RING, device % RING
        if which % 2 == 1:
            along_x = RING - 1 - along_x
        if which // 2 == 1:
            along_z = RING - 1 - along_z
        return along_x * RING + along_z

    adders = tuple(mirror(me, which) for which in range(4))

    barrier = pltpu.get_barrier_semaphore()
    for other in mates[1:] + adders[1:]:
        pl.semaphore_signal(barrier, inc=1, device_id=(other, tens), device_id_type=MESH)
    for other in (up, down, twin):
        pl.semaphore_signal(barrier, inc=1, device_id=(me, other), device_id_type=MESH)

    def lanes(which, width=CHUNK):
        return pl.ds(pl.multiple_of(which * width, width), width)

    def piece_of(device, share):
        return g_ref.at[(device % 2) * 2 + share % 2, :, lanes(device // 2)]

    def own_copy(share):
        return pltpu.make_async_copy(
            piece_of(adders[share // 2], share),
            mt.at[0, :, share * CHUNK : (share + 1) * CHUNK],
            own_sem.at[share],
        )

    for share in range(8):
        own_copy(share).start()

    def cross_copy(mate):
        target = mates[mate]
        along_x, along_z = target // RING, target % RING
        flip_x, flip_z = along_y % 2, along_y // 2
        along_x = along_x + flip_x * (RING - 1 - 2 * along_x)
        along_z = along_z + flip_z * (RING - 1 - 2 * along_z)
        return pltpu.make_async_remote_copy(
            src_ref=piece_of(along_x * RING + along_z, tens),
            dst_ref=mt.at[mate, :, lanes(tens)],
            send_sem=cross_send.at[mate], recv_sem=cross_recv.at[mate],
            device_id=(target, tens), device_id_type=MESH,
        )

    routes = (
        (tens, up, 0, rows),
        (tens, down, 0, rows),
        (tens, twin, 0, rows),
        (down, up, 0, half),
        (down, twin, 0, rows),
        (up, down, half, half),
        (up, twin, 0, rows),
        (far, twin, 0, rows),
    )

    def hop(mate, kind):
        owner, dest, first, count = routes[kind]
        piece = mt.at[mate, pl.ds(first, count), lanes(owner)]
        return pltpu.make_async_remote_copy(
            src_ref=piece, dst_ref=piece,
            send_sem=y_send.at[mate, kind], recv_sem=y_recv.at[mate, kind],
            device_id=(me, dest), device_id_type=MESH,
        )

    def grad_copy(unit, mate, width=HD):
        at = lanes(unit, HD) if width == HD else pl.ds(GQ * HD, width)
        return pltpu.make_async_remote_copy(
            src_ref=grads.at[0, :, at], dst_ref=grads.at[mate, :, at],
            send_sem=grad_send.at[unit, mate], recv_sem=grad_recv.at[unit, mate],
            device_id=(mates[mate], tens), device_id_type=MESH,
        )

    def sum_copy(column, which):
        at = lanes(column)
        return pltpu.make_async_remote_copy(
            src_ref=sums.at[which - 1, :, at], dst_ref=arrived.at[which - 1, :, at],
            send_sem=sum_send.at[column, which], recv_sem=sum_recv.at[column, which],
            device_id=(adders[which], tens), device_id_type=MESH,
        )

    allowed = seg_q_ref[...] == seg_k_ref[...]
    query_at = lax.broadcasted_iota(jnp.int32, bias.shape, 0)
    key_at = lax.broadcasted_iota(jnp.int32, bias.shape, 1)
    bias[...] = jnp.where(allowed & (key_at <= query_at), 0.0, -jnp.inf)
    key_grad[...] = jnp.zeros_like(key_grad)
    value_grad[...] = jnp.zeros_like(value_grad)
    pl.semaphore_wait(barrier, 9)
    for mate in (1, 2, 3):
        cross_copy(mate).start()

    factor = HD ** (-0.5)
    key_cols = pl.ds(GQ * HD, HD)
    value_cols = pl.ds((GQ + 1) * HD, HD)
    across = (((1,), (1,)), ((), ()))
    down_rows = (((0,), (0,)), ((), ()))

    def head(index):
        cols = lanes(index, HD)
        for block in range(2):
            at = pl.ds(block * half, half)
            keys = pl.ds(0, (block + 1) * half)
            query = qkv_ref[at, cols]
            key = qkv_ref[keys, key_cols]
            value = qkv_ref[keys, value_cols]
            grad_out = grad_ref[at, cols]
            scores = lax.dot_general(query, key, across, preferred_element_type=jnp.float32)
            scores = scores * factor + bias[at, keys]
            exponent = jnp.exp(scores - jnp.max(scores, axis=1, keepdims=True))
            prob = exponent * (1.0 / jnp.sum(exponent, axis=1, keepdims=True))
            prob_low = prob.astype(jnp.bfloat16)
            attn_ref[at, cols] = jnp.dot(
                prob_low, value, preferred_element_type=jnp.float32
            ).astype(attn_ref.dtype)
            grad_prob = lax.dot_general(grad_out, value, across, preferred_element_type=jnp.float32)
            row_dot = jnp.sum(prob * grad_prob, axis=1, keepdims=True)
            grad_score = (prob * (grad_prob - row_dot)).astype(jnp.bfloat16)
            grad_query = jnp.dot(grad_score, key, preferred_element_type=jnp.float32) * factor
            grads[0, at, cols] = grad_query.astype(grads.dtype)
            key_grad[keys, :] += lax.dot_general(
                grad_score, query, down_rows, preferred_element_type=jnp.float32
            )
            value_grad[keys, :] += lax.dot_general(
                prob_low, grad_out, down_rows, preferred_element_type=jnp.float32
            )
        for mate in (1, 2, 3):
            grad_copy(index, mate).start()

    def heads(first, count):
        @pl.loop(first, first + count)
        def _(index):
            head(index)

    def turn(mate):
        for share in range(8):
            cols = pl.ds(share * CHUNK, CHUNK)
            mt_t[cols, mate * rows : (mate + 1) * rows] = jnp.transpose(mt[mate, :, cols])

    heads(0, 2)
    for mate in (1, 2, 3):
        cross_copy(mate).wait_recv()
        for kind in (0, 1, 2):
            hop(mate, kind).start()
    heads(2, 2)
    for mate in (1, 2):
        hop(mate, 0).wait_recv()
        hop(mate, 3).start()
        hop(mate, 4).start()
        hop(mate, 1).wait_recv()
        hop(mate, 5).start()
        hop(mate, 6).start()
    heads(4, 2)
    for mate in (3,):
        hop(mate, 0).wait_recv()
        hop(mate, 3).start()
        hop(mate, 4).start()
        hop(mate, 1).wait_recv()
        hop(mate, 5).start()
        hop(mate, 6).start()
    heads(6, 2)
    grads[0, :, key_cols] = (key_grad[...] * factor).astype(grads.dtype)
    grads[0, :, value_cols] = value_grad[...].astype(grads.dtype)
    for mate in (1, 2, 3):
        grad_copy(GQ, mate, 2 * HD).start()
    for share in range(8):
        own_copy(share).wait()
    turn(0)
    for mate in (1, 2, 3):
        hop(mate, 3).wait_recv()
        hop(mate, 5).wait_recv()
        hop(mate, 7).start()
    for mate in (1, 2, 3):
        for kind in (2, 4, 6, 7):
            hop(mate, kind).wait_recv()
        turn(mate)

    wide = mt_t.shape[0] // 4
    for column in range(weight_grad_ref.shape[1] // CHUNK):
        for mate in (1, 2, 3):
            if column < GQ // 2:
                grad_copy(2 * column, mate).wait_recv()
                grad_copy(2 * column + 1, mate).wait_recv()
            else:
                grad_copy(GQ, mate, 2 * HD).wait_recv()
        at = pl.ds(column * CHUNK, CHUNK)
        right = grads[:, :, at].reshape(4 * rows, CHUNK)
        for which in (3, 1, 2, 0):
            left = mt_t[which * wide : (which + 1) * wide, :]
            term = jnp.dot(left, right, preferred_element_type=jnp.float32)
            if which == 0:
                weight_grad_ref[:, at] = term
            else:
                sums[which - 1, :, at] = term.astype(sums.dtype)
                sum_copy(column, which).start()
    for column in range(weight_grad_ref.shape[1] // CHUNK):
        at = pl.ds(column * CHUNK, CHUNK)
        for which in (1, 2, 3):
            sum_copy(column, which).wait_recv()
        total = weight_grad_ref[:, at]
        for which in (1, 2, 3):
            total = total + arrived[which - 1, :, at].astype(jnp.float32)
        weight_grad_ref[:, at] = total

    for mate in (1, 2, 3):
        cross_copy(mate).wait_send()
        for kind in range(len(routes)):
            hop(mate, kind).wait_send()
        for index in range(GQ):
            grad_copy(index, mate).wait_send()
        grad_copy(GQ, mate, 2 * HD).wait_send()
        for column in range(weight_grad_ref.shape[1] // CHUNK):
            sum_copy(column, mate).wait_send()


def backward_call(qkv, out_grad, segment, pieces):
    rows, columns = qkv.shape
    wide = 4 * rows
    low = jnp.bfloat16
    return pl.pallas_call(
        backward_kernel,
        out_shape=(
            jax.ShapeDtypeStruct(out_grad.shape, low),
            jax.ShapeDtypeStruct((rows, columns), jnp.float32),
        ),
        in_specs=[pl.BlockSpec(memory_space=pltpu.VMEM)] * 4 + [pl.BlockSpec(memory_space=pl.ANY)],
        out_specs=(pl.BlockSpec(memory_space=pltpu.VMEM), pl.BlockSpec(memory_space=pltpu.VMEM)),
        scratch_shapes=[
            pltpu.VMEM((4, rows, wide), low),
            pltpu.VMEM((wide, 4 * rows), low),
            pltpu.VMEM((4, rows, columns), low),
            pltpu.VMEM((3, rows, columns), low),
            pltpu.VMEM((3, rows, columns), low),
            pltpu.VMEM((rows, rows), jnp.float32),
            pltpu.VMEM((rows, HD), jnp.float32),
            pltpu.VMEM((rows, HD), jnp.float32),
            pltpu.SemaphoreType.DMA((8,)),
            pltpu.SemaphoreType.DMA((4,)),
            pltpu.SemaphoreType.DMA((4,)),
            pltpu.SemaphoreType.DMA((4, 8)),
            pltpu.SemaphoreType.DMA((4, 8)),
            pltpu.SemaphoreType.DMA((GQ + 1, 4)),
            pltpu.SemaphoreType.DMA((GQ + 1, 4)),
            pltpu.SemaphoreType.DMA((5, 4)),
            pltpu.SemaphoreType.DMA((5, 4)),
        ],
        compiler_params=pltpu.CompilerParams(
            collective_id=1, has_side_effects=True, vmem_limit_bytes=56 * 2**20
        ),
        cost_estimate=pl.CostEstimate(
            flops=2 * wide * wide * columns, bytes_accessed=20 * 2**20, transcendentals=GQ * rows * rows
        ),
    )(qkv, out_grad, segment[:, None], segment[None, :], pieces)


def local(tokens, block_target, doc_lengths, qkv_weight, out_grad):
    tok_dev = tokens.shape[0]
    qkv, pieces = forward_call(block_target, tokens, qkv_weight, lax.axis_size("dp"))
    doc_ends = jnp.cumsum(doc_lengths[0])
    position = jnp.arange(tok_dev, dtype=jnp.int32)
    segment = jnp.sum((position[:, None] >= doc_ends[None, :]).astype(jnp.int32), axis=1)
    return backward_call(qkv, out_grad, segment, pieces)


def solution(mesh):
    placed = (P("dp", "tensor"), P("dp"), P("dp", None), P(None, "tensor"), P("dp", "tensor"))
    return jax.shard_map(
        local,
        mesh=mesh,
        in_specs=placed,
        out_specs=(P("dp", "tensor"), P("dp", "tensor")),
        check_vma=False,
    )
```

```python
import jax
import jax.numpy as jnp
from jax import lax
from jax.experimental import pallas as pl
from jax.experimental.pallas import tpu as pltpu
from jax.sharding import PartitionSpec as P

HD = 128
GQ = 8
BLK = 128
RING = 4
CHUNK = 256
MESH = pl.DeviceIdType.MESH


def peer_at(me, step):
    along_x = (me // RING + step // RING) % RING
    along_z = (me % RING + step % RING) % RING
    return along_x * RING + along_z


def step_kernel(
    target_ref, docs_ref, tok_ref, w_ref, grad_ref, attn_ref, weight_grad_ref,
    tag_out, tags, tags_smem, out_buf, arr0, arr1, arr2, arr3, g, w_buf, qkv,
    mt, grads, sums, summed, bias, key_grad, value_grad,
    tag_send, tag_recv, move_send, move_recv, y_send, y_recv, w_sem, smem_sem,
    cross_send, cross_recv, m_send, m_recv, grad_send, grad_recv, sum_send, sum_recv,
):
    arrived = (arr0, arr1, arr2, arr3)
    parts = len(arrived)
    blocks = tok_ref.shape[0]
    peers = tags.shape[0]
    rows = blocks * BLK
    half = rows // 2
    columns = weight_grad_ref.shape[1] // CHUNK
    me = lax.axis_index("dp")
    tens = lax.axis_index("tensor")
    at_x, at_z = me // RING, me % RING
    along_y, core = tens // 2, tens % 2
    up = ((along_y + 1) % RING) * 2 + core
    down = ((along_y + RING - 1) % RING) * 2 + core
    far = ((along_y + 2) % RING) * 2 + core
    twin = along_y * 2 + 1 - core
    near_x = at_x + 1 - 2 * (at_x % 2)
    near_z = at_z + 1 - 2 * (at_z % 2)
    mates = ((at_x, at_z), (near_x, at_z), (at_x, near_z), (near_x, near_z))
    adders = (
        me,
        (RING - 1 - at_x) * RING + at_z,
        at_x * RING + RING - 1 - at_z,
        (RING - 1 - at_x) * RING + RING - 1 - at_z,
    )

    def mate_id(mate):
        return mates[mate][0] * RING + mates[mate][1]

    def lanes(which, width=CHUNK):
        return pl.ds(pl.multiple_of(which * width, width), width)

    def weight_copy(part):
        return pltpu.make_async_copy(w_ref.at[:, part], w_buf.at[part], w_sem.at[part])

    for part in range(parts):
        weight_copy(part).start()

    row_of = lax.broadcasted_iota(jnp.int32, tag_out.shape, 0)
    tile = jnp.zeros(tag_out.shape, jnp.int32)
    for slot in range(blocks):
        tile = jnp.where(row_of == slot, target_ref[slot], tile)
    tag_out[...] = tile

    barrier = pltpu.get_barrier_semaphore()

    @pl.loop(1, peers)
    def _(step):
        pl.semaphore_signal(barrier, inc=1, device_id=(peer_at(me, step), tens), device_id_type=MESH)

    for other in (up, down, twin):
        pl.semaphore_signal(barrier, inc=1, device_id=(me, other), device_id_type=MESH)

    def block_for(peer):
        picked = jnp.int32(0)
        for slot in range(blocks):
            picked = jnp.where(target_ref[slot] // blocks == peer, slot, picked)
        return picked

    def pack(part):
        @pl.loop(0, peers)
        def _(peer):
            out_buf[part, peer] = tok_ref[block_for(peer), :, part * CHUNK : (part + 1) * CHUNK]

    def tag_copy(step):
        return pltpu.make_async_remote_copy(
            src_ref=tag_out, dst_ref=tags.at[me],
            send_sem=tag_send.at[step], recv_sem=tag_recv.at[step],
            device_id=(peer_at(me, step), tens), device_id_type=MESH,
        )

    def move_copy(part, step):
        peer = peer_at(me, step)
        return pltpu.make_async_remote_copy(
            src_ref=out_buf.at[part, peer], dst_ref=arrived[part].at[me],
            send_sem=move_send.at[part, step], recv_sem=move_recv.at[part, step],
            device_id=(peer, tens), device_id_type=MESH,
        )

    def send_part(part):
        @pl.loop(1, peers)
        def _(step):
            move_copy(part, step).start()

        arrived[part][me] = out_buf[part, me]

    pack(0)
    pl.semaphore_wait(barrier, peers - 1 + 3)

    @pl.loop(1, peers)
    def _(step):
        tag_copy(step).start()

    send_part(0)
    for part in range(1, parts):
        pack(part)
        send_part(part)
    tags[me] = tag_out[...]

    query_at = lax.broadcasted_iota(jnp.int32, bias.shape, 0)
    key_at = lax.broadcasted_iota(jnp.int32, bias.shape, 1)
    allowed = key_at <= query_at
    doc_end = jnp.int32(0)
    for doc in range(docs_ref.shape[1]):
        doc_end = doc_end + docs_ref[0, doc]
        allowed = allowed & ((query_at >= doc_end) == (key_at >= doc_end))
    bias[...] = jnp.where(allowed, 0.0, -jnp.inf).astype(bias.dtype)
    key_grad[...] = jnp.zeros_like(key_grad)
    value_grad[...] = jnp.zeros_like(value_grad)

    @pl.loop(1, peers)
    def _(step):
        tag_copy(step).wait()

    to_smem = pltpu.make_async_copy(tags, tags_smem, smem_sem)
    to_smem.start()
    to_smem.wait()

    def source_of(slot):
        def look(peer, found):
            for entry in range(blocks):
                found = jnp.where(tags_smem[peer, entry, 0] == me * blocks + slot, peer, found)
            return found

        return lax.fori_loop(0, peers, look, jnp.int32(0))

    sources = [source_of(slot) for slot in range(blocks)]

    def ring_routes(count):
        return (
            (tens, up, 0, count),
            (tens, down, 0, count),
            (tens, twin, 0, count),
            (down, up, 0, count // 2),
            (down, twin, 0, count),
            (up, down, count // 2, count // 2),
            (up, twin, 0, count),
            (far, twin, 0, count),
        )

    share = rows // 8
    token_routes = ring_routes(rows)
    moved_routes = ring_routes(share)

    def token_hop(part, kind):
        owner, dest, first, count = token_routes[kind]
        piece = g.at[part, pl.ds(first, count), lanes(owner)]
        return pltpu.make_async_remote_copy(
            src_ref=piece, dst_ref=piece,
            send_sem=y_send.at[part, kind], recv_sem=y_recv.at[part, kind],
            device_id=(me, dest), device_id_type=MESH,
        )

    def moved_hop(part, kind):
        owner, dest, first, count = moved_routes[kind]
        at = pl.ds(pl.multiple_of(owner * share + first, 16), count)
        piece = mt.at[part, at, pl.ds(0, 6 * CHUNK)]
        return pltpu.make_async_remote_copy(
            src_ref=piece, dst_ref=piece,
            send_sem=m_send.at[part, kind], recv_sem=m_recv.at[part, kind],
            device_id=(me, dest), device_id_type=MESH,
        )

    def begin(hop, part):
        for kind in (0, 1, 2):
            hop(part, kind).start()

    def onward(hop, part):
        hop(part, 0).wait_recv()
        hop(part, 3).start()
        hop(part, 4).start()
        hop(part, 1).wait_recv()
        hop(part, 5).start()
        hop(part, 6).start()

    def last(hop, part):
        hop(part, 3).wait_recv()
        hop(part, 5).wait_recv()
        hop(part, 7).start()

    def complete(hop, part):
        for kind in (2, 4, 6, 7):
            hop(part, kind).wait_recv()

    def slice_of(device, part, flip):
        along_x, along_z = device
        along_x = RING - 1 - along_x if flip else along_x
        along_z = along_z + (RING - 1 - 2 * along_z) * ((along_z + part // 2) % 2)
        return lanes(along_x * 2 + along_z // 2)

    def cross_copy(part, mate, flip):
        at = pl.ds(pl.multiple_of(tens * share, share), share)
        return pltpu.make_async_remote_copy(
            src_ref=g.at[part, at, slice_of(mates[mate], part, flip)],
            dst_ref=mt.at[part, at, pl.ds((2 * mate - 2 + flip) * CHUNK, CHUNK)],
            send_sem=cross_send.at[part, mate, flip], recv_sem=cross_recv.at[part, mate, flip],
            device_id=(mate_id(mate), tens), device_id_type=MESH,
        )

    def cross_start(part):
        for mate in (1, 2, 3):
            for flip in range(2):
                cross_copy(part, mate, flip).start()

    def moved_begin(part):
        for mate in (1, 2, 3):
            for flip in range(2):
                cross_copy(part, mate, flip).wait_recv()
        begin(moved_hop, part)

    def multiply(part):
        weight_copy(part).wait()

        @pl.loop(0, columns)
        def _(column):
            at = lanes(column)
            weights = w_buf[part, :, :, at].reshape(g.shape[2], CHUNK)
            term = jnp.dot(g[part], weights, preferred_element_type=jnp.float32)
            if part == 0:
                weight_grad_ref[:, at] = term
            elif part < parts - 1:
                weight_grad_ref[:, at] += term
            else:
                qkv[:, at] = (weight_grad_ref[:, at] + term).astype(qkv.dtype)

    for part in range(parts):
        @pl.loop(1, peers)
        def _(step):
            move_copy(part, step).wait_recv()

        for slot in range(blocks):
            g[part, slot * BLK : (slot + 1) * BLK, lanes(tens)] = arrived[part][sources[slot]]
        begin(token_hop, part)
        if part > 0:
            complete(token_hop, part - 1)
            cross_start(part - 1)
            multiply(part - 1)
        onward(token_hop, part)
        if part == 2:
            moved_begin(0)
        if part == 3:
            onward(moved_hop, 0)
            moved_begin(1)
        last(token_hop, part)
    complete(token_hop, parts - 1)
    cross_start(parts - 1)
    multiply(parts - 1)

    factor = HD ** (-0.5)
    key_cols = pl.ds(GQ * HD, HD)
    value_cols = pl.ds((GQ + 1) * HD, HD)
    across = (((1,), (1,)), ((), ()))
    down_rows = (((0,), (0,)), ((), ()))

    def head(pair, which):
        cols = lanes(2 * pair + which, HD)
        for block in range(2):
            at = pl.ds(block * half, half)
            keys = pl.ds(0, (block + 1) * half)
            query = qkv[at, cols]
            key = qkv[keys, key_cols]
            value = qkv[keys, value_cols]
            grad_out = grad_ref[at, cols]
            scores = lax.dot_general(query, key, across, preferred_element_type=jnp.float32)
            scores = scores * factor + bias[at, keys].astype(jnp.float32)
            exponent = jnp.exp(scores - jnp.max(scores, axis=1, keepdims=True))
            prob = exponent * (1.0 / jnp.sum(exponent, axis=1, keepdims=True))
            prob_low = prob.astype(jnp.bfloat16)
            attn_ref[at, cols] = jnp.dot(
                prob_low, value, preferred_element_type=jnp.float32
            ).astype(attn_ref.dtype)
            grad_prob = lax.dot_general(grad_out, value, across, preferred_element_type=jnp.float32)
            row_dot = jnp.sum(prob * grad_prob, axis=1, keepdims=True)
            grad_score = (prob * (grad_prob - row_dot)).astype(jnp.bfloat16)
            grad_query = jnp.dot(grad_score, key, preferred_element_type=jnp.float32) * factor
            grads[0, pair, at, lanes(which, HD)] = grad_query.astype(grads.dtype)
            key_grad[keys, :] += lax.dot_general(
                grad_score, query, down_rows, preferred_element_type=jnp.float32
            )
            value_grad[keys, :] += lax.dot_general(
                prob_low, grad_out, down_rows, preferred_element_type=jnp.float32
            )

    def heads(pair):
        for which in range(2):
            head(pair, which)

    grad_routes = ((0, 1, 1, 0, rows), (0, 2, 2, 0, rows), (1, 2, 3, 0, half), (2, 1, 3, half, half))

    def grad_copy(pair, kind):
        source, mate, slot, first, count = grad_routes[kind]
        return pltpu.make_async_remote_copy(
            src_ref=grads.at[source, pair, pl.ds(first, count)],
            dst_ref=grads.at[slot, pair, pl.ds(first, count)],
            send_sem=grad_send.at[pair, kind], recv_sem=grad_recv.at[pair, kind],
            device_id=(mate_id(mate), tens), device_id_type=MESH,
        )

    def grad_begin(pair):
        grad_copy(pair, 0).start()
        grad_copy(pair, 1).start()

    def grad_onward(pair):
        grad_copy(pair, 0).wait_recv()
        grad_copy(pair, 2).start()
        grad_copy(pair, 1).wait_recv()
        grad_copy(pair, 3).start()

    def grad_complete(pair):
        grad_copy(pair, 2).wait_recv()
        grad_copy(pair, 3).wait_recv()

    last(moved_hop, 0)
    onward(moved_hop, 1)
    moved_begin(2)
    heads(0)
    grad_begin(0)
    last(moved_hop, 1)
    onward(moved_hop, 2)
    moved_begin(3)
    heads(1)
    grad_begin(1)
    last(moved_hop, 2)
    onward(moved_hop, 3)
    heads(2)
    grad_begin(2)
    grad_onward(0)
    last(moved_hop, 3)
    heads(3)
    grad_begin(3)
    grads[0, GQ // 2, :, :HD] = (key_grad[...] * factor).astype(grads.dtype)
    grads[0, GQ // 2, :, HD:] = value_grad[...].astype(grads.dtype)
    grad_begin(4)
    grad_onward(1)

    for part in range(parts):
        complete(moved_hop, part)
        for kind in range(8):
            token_hop(part, kind).wait_send()
            moved_hop(part, kind).wait_send()
        for mate in (1, 2, 3):
            for flip in range(2):
                cross_copy(part, mate, flip).wait_send()

        @pl.loop(1, peers)
        def _(step):
            move_copy(part, step).wait_send()

    def side_term(which, column):
        parity = (at_z + which // 2) % 2
        terms = []
        for side in range(2):
            total = None
            for mate in range(4):
                if mate == 0:
                    along_z = at_z if which < 2 else RING - 1 - at_z
                    along_x = at_x if which % 2 == 0 else RING - 1 - at_x
                    left = g[2 * parity + side, :, lanes(along_x * 2 + along_z // 2)]
                else:
                    left = mt[2 * parity + side, :, pl.ds((2 * mate - 2 + which % 2) * CHUNK, CHUNK)]
                term = lax.dot_general(
                    left, grads[mate, column], down_rows, preferred_element_type=jnp.float32
                )
                total = term if total is None else total + term
            terms.append(total)
        return jnp.concatenate(terms, axis=0)

    def sum_copy(column, which):
        return pltpu.make_async_remote_copy(
            src_ref=sums.at[which - 1, column], dst_ref=summed.at[which - 1, column],
            send_sem=sum_send.at[column, which], recv_sem=sum_recv.at[column, which],
            device_id=(adders[which], tens), device_id_type=MESH,
        )

    def sum_complete(column):
        at = pl.ds(column * CHUNK, CHUNK)
        total = weight_grad_ref[:, at]
        for which in (1, 2, 3):
            sum_copy(column, which).wait_recv()
            total = total + summed[which - 1, column].astype(jnp.float32)
        weight_grad_ref[:, at] = total

    for column in range(columns):
        grad_complete(column)
        at = pl.ds(column * CHUNK, CHUNK)
        for which in (3, 2, 1, 0):
            term = side_term(which, column)
            if which == 0:
                weight_grad_ref[:, at] = term
            else:
                sums[which - 1, column] = term.astype(sums.dtype)
                sum_copy(column, which).start()
        if column >= 1 and column + 1 < columns:
            grad_onward(column + 1)
    for column in range(columns):
        sum_complete(column)

    for column in range(columns):
        for kind in range(len(grad_routes)):
            grad_copy(column, kind).wait_send()
        for which in (1, 2, 3):
            sum_copy(column, which).wait_send()


def local(tokens, block_target, doc_lengths, qkv_weight, out_grad):
    peers = lax.axis_size("dp")
    rows, width = tokens.shape
    blocks = rows // BLK
    parts = width // CHUNK
    depth, columns = qkv_weight.shape
    tensors = depth // width
    wide = depth // parts
    pairs = columns // CHUNK
    low = jnp.bfloat16
    dma = pltpu.SemaphoreType.DMA
    vmem = pl.BlockSpec(memory_space=pltpu.VMEM)
    smem = pl.BlockSpec(memory_space=pltpu.SMEM)
    return pl.pallas_call(
        step_kernel,
        out_shape=(
            jax.ShapeDtypeStruct(out_grad.shape, low),
            jax.ShapeDtypeStruct((rows, columns), jnp.float32),
        ),
        in_specs=[smem, smem, vmem, pl.BlockSpec(memory_space=pl.ANY), vmem],
        out_specs=(vmem, vmem),
        scratch_shapes=[
            pltpu.VMEM((8, 128), jnp.int32),
            pltpu.VMEM((peers, 8, 128), jnp.int32),
            pltpu.SMEM((peers, 8, 128), jnp.int32),
            pltpu.VMEM((parts, peers, BLK, CHUNK), low),
            *[pltpu.VMEM((peers, BLK, CHUNK), low) for _ in range(parts)],
            pltpu.VMEM((parts, rows, wide), low),
            pltpu.VMEM((parts, tensors, CHUNK, columns), low),
            pltpu.VMEM((rows, columns), low),
            pltpu.VMEM((parts, rows, 6 * CHUNK), low),
            pltpu.VMEM((4, pairs, rows, CHUNK), low),
            pltpu.VMEM((3, pairs, rows, CHUNK), low),
            pltpu.VMEM((3, pairs, rows, CHUNK), low),
            pltpu.VMEM((rows, rows), low),
            pltpu.VMEM((rows, HD), jnp.float32),
            pltpu.VMEM((rows, HD), jnp.float32),
            dma((peers,)), dma((peers,)),
            dma((parts, peers)), dma((parts, peers)),
            dma((parts, 8)), dma((parts, 8)),
            dma((parts,)), dma,
            dma((parts, 4, 2)), dma((parts, 4, 2)),
            dma((parts, 8)), dma((parts, 8)),
            dma((pairs, 4)), dma((pairs, 4)),
            dma((pairs, 4)), dma((pairs, 4)),
        ],
        compiler_params=pltpu.CompilerParams(
            collective_id=0, has_side_effects=True, vmem_limit_bytes=64 * 2**20
        ),
    )(
        block_target,
        doc_lengths,
        tokens.reshape(blocks, BLK, width),
        qkv_weight.reshape(tensors, parts, CHUNK, columns),
        out_grad,
    )


def solution(mesh):
    placed = (P("dp", "tensor"), P("dp"), P("dp", None), P(None, "tensor"), P("dp", "tensor"))
    return jax.shard_map(
        local,
        mesh=mesh,
        in_specs=placed,
        out_specs=(P("dp", "tensor"), P("dp", "tensor")),
        check_vma=False,
    )
```

```python
import jax
import jax.numpy as jnp
from jax import lax
from jax.experimental import pallas as pl
from jax.experimental.pallas import tpu as pltpu
from jax.sharding import PartitionSpec as P

HD = 128
GQ = 8
BLK = 128
RING = 4
CHUNK = 256
MESH = pl.DeviceIdType.MESH


def peer_at(me, step):
    along_x = (me // RING + step // RING) % RING
    along_z = (me % RING + step % RING) % RING
    return along_x * RING + along_z


def step_kernel(
    target_ref, docs_ref, tok_ref, w_ref, grad_ref, attn_ref, weight_grad_ref,
    tag_out, tags, tags_smem, out_buf, arr0, arr1, arr2, arr3, g, w_buf, qkv,
    mt, grads, diag, soon, late, relay, summed, bias, key_grad, value_grad,
    tag_send, tag_recv, move_send, move_recv, y_send, y_recv, w_sem, smem_sem,
    cross_send, cross_recv, m_send, m_recv, grad_send, grad_recv, sum_send, sum_recv,
):
    arrived = (arr0, arr1, arr2, arr3)
    parts = len(arrived)
    blocks = tok_ref.shape[0]
    peers = tags.shape[0]
    rows = blocks * BLK
    half = rows // 2
    columns = weight_grad_ref.shape[1] // CHUNK
    me = lax.axis_index("dp")
    tens = lax.axis_index("tensor")
    at_x, at_z = me // RING, me % RING
    along_y, core = tens // 2, tens % 2
    up = ((along_y + 1) % RING) * 2 + core
    down = ((along_y + RING - 1) % RING) * 2 + core
    far = ((along_y + 2) % RING) * 2 + core
    twin = along_y * 2 + 1 - core
    near_x = at_x + 1 - 2 * (at_x % 2)
    near_z = at_z + 1 - 2 * (at_z % 2)
    mates = ((at_x, at_z), (near_x, at_z), (at_x, near_z), (near_x, near_z))
    adders = (
        me,
        (RING - 1 - at_x) * RING + at_z,
        at_x * RING + RING - 1 - at_z,
        (RING - 1 - at_x) * RING + RING - 1 - at_z,
    )

    def mate_id(mate):
        return mates[mate][0] * RING + mates[mate][1]

    def lanes(which, width=CHUNK):
        return pl.ds(pl.multiple_of(which * width, width), width)

    def weight_copy(part):
        return pltpu.make_async_copy(w_ref.at[:, part], w_buf.at[part], w_sem.at[part])

    for part in range(parts):
        weight_copy(part).start()

    row_of = lax.broadcasted_iota(jnp.int32, tag_out.shape, 0)
    tile = jnp.zeros(tag_out.shape, jnp.int32)
    for slot in range(blocks):
        tile = jnp.where(row_of == slot, target_ref[slot], tile)
    tag_out[...] = tile

    barrier = pltpu.get_barrier_semaphore()

    @pl.loop(1, peers)
    def _(step):
        pl.semaphore_signal(barrier, inc=1, device_id=(peer_at(me, step), tens), device_id_type=MESH)

    for other in (up, down, twin):
        pl.semaphore_signal(barrier, inc=1, device_id=(me, other), device_id_type=MESH)

    def block_for(peer):
        picked = jnp.int32(0)
        for slot in range(blocks):
            picked = jnp.where(target_ref[slot] // blocks == peer, slot, picked)
        return picked

    def pack(part):
        @pl.loop(0, peers)
        def _(peer):
            out_buf[part, peer] = tok_ref[block_for(peer), :, part * CHUNK : (part + 1) * CHUNK]

    def tag_copy(step):
        return pltpu.make_async_remote_copy(
            src_ref=tag_out, dst_ref=tags.at[me],
            send_sem=tag_send.at[step], recv_sem=tag_recv.at[step],
            device_id=(peer_at(me, step), tens), device_id_type=MESH,
        )

    def move_copy(part, step):
        peer = peer_at(me, step)
        return pltpu.make_async_remote_copy(
            src_ref=out_buf.at[part, peer], dst_ref=arrived[part].at[me],
            send_sem=move_send.at[part, step], recv_sem=move_recv.at[part, step],
            device_id=(peer, tens), device_id_type=MESH,
        )

    def send_part(part):
        @pl.loop(1, peers)
        def _(step):
            move_copy(part, step).start()

        arrived[part][me] = out_buf[part, me]

    pack(0)
    pl.semaphore_wait(barrier, peers - 1 + 3)

    @pl.loop(1, peers)
    def _(step):
        tag_copy(step).start()

    send_part(0)
    for part in range(1, parts):
        pack(part)
        send_part(part)
    tags[me] = tag_out[...]

    query_at = lax.broadcasted_iota(jnp.int32, bias.shape, 0)
    key_at = lax.broadcasted_iota(jnp.int32, bias.shape, 1)
    allowed = key_at <= query_at
    doc_end = jnp.int32(0)
    for doc in range(docs_ref.shape[1]):
        doc_end = doc_end + docs_ref[0, doc]
        allowed = allowed & ((query_at >= doc_end) == (key_at >= doc_end))
    bias[...] = jnp.where(allowed, 0.0, -jnp.inf).astype(bias.dtype)
    key_grad[...] = jnp.zeros_like(key_grad)
    value_grad[...] = jnp.zeros_like(value_grad)

    @pl.loop(1, peers)
    def _(step):
        tag_copy(step).wait()

    to_smem = pltpu.make_async_copy(tags, tags_smem, smem_sem)
    to_smem.start()
    to_smem.wait()

    def source_of(slot):
        def look(peer, found):
            for entry in range(blocks):
                found = jnp.where(tags_smem[peer, entry, 0] == me * blocks + slot, peer, found)
            return found

        return lax.fori_loop(0, peers, look, jnp.int32(0))

    sources = [source_of(slot) for slot in range(blocks)]

    def ring_routes(count):
        return (
            (tens, up, 0, count),
            (tens, down, 0, count),
            (tens, twin, 0, count),
            (down, up, 0, count // 2),
            (down, twin, 0, count),
            (up, down, count // 2, count // 2),
            (up, twin, 0, count),
            (far, twin, 0, count),
        )

    share = rows // 8
    token_routes = ring_routes(rows)
    moved_routes = ring_routes(share)

    def token_hop(part, kind):
        owner, dest, first, count = token_routes[kind]
        piece = g.at[part, pl.ds(first, count), lanes(owner)]
        return pltpu.make_async_remote_copy(
            src_ref=piece, dst_ref=piece,
            send_sem=y_send.at[part, kind], recv_sem=y_recv.at[part, kind],
            device_id=(me, dest), device_id_type=MESH,
        )

    def moved_hop(part, kind):
        owner, dest, first, count = moved_routes[kind]
        at = pl.ds(pl.multiple_of(owner * share + first, 16), count)
        piece = mt.at[part, at, pl.ds(0, 6 * CHUNK)]
        return pltpu.make_async_remote_copy(
            src_ref=piece, dst_ref=piece,
            send_sem=m_send.at[part, kind], recv_sem=m_recv.at[part, kind],
            device_id=(me, dest), device_id_type=MESH,
        )

    def begin(hop, part):
        for kind in (0, 1, 2):
            hop(part, kind).start()

    def onward(hop, part):
        hop(part, 0).wait_recv()
        hop(part, 3).start()
        hop(part, 4).start()
        hop(part, 1).wait_recv()
        hop(part, 5).start()
        hop(part, 6).start()

    def last(hop, part):
        hop(part, 3).wait_recv()
        hop(part, 5).wait_recv()
        hop(part, 7).start()

    def complete(hop, part):
        for kind in (2, 4, 6, 7):
            hop(part, kind).wait_recv()

    def slice_of(device, part, flip):
        along_x, along_z = device
        along_x = RING - 1 - along_x if flip else along_x
        along_z = along_z + (RING - 1 - 2 * along_z) * ((along_z + part // 2) % 2)
        return lanes(along_x * 2 + along_z // 2)

    def cross_copy(part, mate, flip):
        at = pl.ds(pl.multiple_of(tens * share, share), share)
        return pltpu.make_async_remote_copy(
            src_ref=g.at[part, at, slice_of(mates[mate], part, flip)],
            dst_ref=mt.at[part, at, pl.ds((2 * mate - 2 + flip) * CHUNK, CHUNK)],
            send_sem=cross_send.at[part, mate, flip], recv_sem=cross_recv.at[part, mate, flip],
            device_id=(mate_id(mate), tens), device_id_type=MESH,
        )

    def cross_start(part):
        for mate in (1, 2, 3):
            for flip in range(2):
                cross_copy(part, mate, flip).start()

    def moved_begin(part):
        for mate in (1, 2, 3):
            for flip in range(2):
                cross_copy(part, mate, flip).wait_recv()
        begin(moved_hop, part)

    def multiply(part):
        weight_copy(part).wait()

        @pl.loop(0, columns)
        def _(column):
            at = lanes(column)
            weights = w_buf[part, :, :, at].reshape(g.shape[2], CHUNK)
            term = jnp.dot(g[part], weights, preferred_element_type=jnp.float32)
            if part == 0:
                weight_grad_ref[:, at] = term
            elif part < parts - 1:
                weight_grad_ref[:, at] += term
            else:
                qkv[:, at] = (weight_grad_ref[:, at] + term).astype(qkv.dtype)

    for part in range(parts):
        @pl.loop(1, peers)
        def _(step):
            move_copy(part, step).wait_recv()

        for slot in range(blocks):
            g[part, slot * BLK : (slot + 1) * BLK, lanes(tens)] = arrived[part][sources[slot]]
        begin(token_hop, part)
        if part > 1:
            last(moved_hop, part - 2)
        if part > 0:
            complete(token_hop, part - 1)
            cross_start(part - 1)
            multiply(part - 1)
        onward(token_hop, part)
        if part > 0:
            moved_begin(part - 1)
        last(token_hop, part)
        if 0 < part < parts - 1:
            onward(moved_hop, part - 1)
    complete(token_hop, parts - 1)
    cross_start(parts - 1)
    onward(moved_hop, parts - 2)
    multiply(parts - 1)

    factor = HD ** (-0.5)
    key_cols = pl.ds(GQ * HD, HD)
    value_cols = pl.ds((GQ + 1) * HD, HD)
    across = (((1,), (1,)), ((), ()))
    down_rows = (((0,), (0,)), ((), ()))

    def head(pair, which):
        cols = lanes(2 * pair + which, HD)
        for block in range(2):
            at = pl.ds(block * half, half)
            keys = pl.ds(0, (block + 1) * half)
            query = qkv[at, cols]
            key = qkv[keys, key_cols]
            value = qkv[keys, value_cols]
            grad_out = grad_ref[at, cols]
            scores = lax.dot_general(query, key, across, preferred_element_type=jnp.float32)
            scores = scores * factor + bias[at, keys].astype(jnp.float32)
            exponent = jnp.exp(scores - jnp.max(scores, axis=1, keepdims=True))
            prob = exponent * (1.0 / jnp.sum(exponent, axis=1, keepdims=True))
            prob_low = prob.astype(jnp.bfloat16)
            attn_ref[at, cols] = jnp.dot(
                prob_low, value, preferred_element_type=jnp.float32
            ).astype(attn_ref.dtype)
            grad_prob = lax.dot_general(grad_out, value, across, preferred_element_type=jnp.float32)
            row_dot = jnp.sum(prob * grad_prob, axis=1, keepdims=True)
            grad_score = (prob * (grad_prob - row_dot)).astype(jnp.bfloat16)
            grad_query = jnp.dot(grad_score, key, preferred_element_type=jnp.float32) * factor
            grads[0, pair, at, lanes(which, HD)] = grad_query.astype(grads.dtype)
            key_grad[keys, :] += lax.dot_general(
                grad_score, query, down_rows, preferred_element_type=jnp.float32
            )
            value_grad[keys, :] += lax.dot_general(
                prob_low, grad_out, down_rows, preferred_element_type=jnp.float32
            )

    def heads(pair):
        for which in range(2):
            head(pair, which)

    grad_routes = ((0, 1, 1, 0, rows), (0, 2, 2, 0, rows), (1, 2, 3, 0, half), (2, 1, 3, half, half))

    def grad_copy(pair, kind):
        source, mate, slot, first, count = grad_routes[kind]
        return pltpu.make_async_remote_copy(
            src_ref=grads.at[source, pair, pl.ds(first, count)],
            dst_ref=grads.at[slot, pair, pl.ds(first, count)],
            send_sem=grad_send.at[pair, kind], recv_sem=grad_recv.at[pair, kind],
            device_id=(mate_id(mate), tens), device_id_type=MESH,
        )

    def grad_begin(pair):
        grad_copy(pair, 0).start()
        grad_copy(pair, 1).start()

    def grad_onward(pair):
        grad_copy(pair, 0).wait_recv()
        grad_copy(pair, 2).start()
        grad_copy(pair, 1).wait_recv()
        grad_copy(pair, 3).start()

    def grad_complete(pair):
        grad_copy(pair, 2).wait_recv()
        grad_copy(pair, 3).wait_recv()

    moved_begin(parts - 1)
    last(moved_hop, parts - 2)
    heads(0)
    grad_begin(0)
    onward(moved_hop, parts - 1)
    heads(1)
    grad_begin(1)
    last(moved_hop, parts - 1)
    heads(2)
    grad_begin(2)
    grad_onward(0)
    heads(3)
    grad_begin(3)
    grads[0, GQ // 2, :, :HD] = (key_grad[...] * factor).astype(grads.dtype)
    grads[0, GQ // 2, :, HD:] = value_grad[...].astype(grads.dtype)
    grad_begin(4)
    grad_onward(1)

    for part in range(parts):
        complete(moved_hop, part)
        for kind in range(8):
            token_hop(part, kind).wait_send()
            moved_hop(part, kind).wait_send()
        for mate in (1, 2, 3):
            for flip in range(2):
                cross_copy(part, mate, flip).wait_send()

        @pl.loop(1, peers)
        def _(step):
            move_copy(part, step).wait_send()

    def side_term(which, column):
        parity = (at_z + which // 2) % 2
        terms = []
        for side in range(2):
            total = None
            for mate in range(4):
                if mate == 0:
                    along_z = at_z if which < 2 else RING - 1 - at_z
                    along_x = at_x if which % 2 == 0 else RING - 1 - at_x
                    left = g[2 * parity + side, :, lanes(along_x * 2 + along_z // 2)]
                else:
                    left = mt[2 * parity + side, :, pl.ds((2 * mate - 2 + which % 2) * CHUNK, CHUNK)]
                term = lax.dot_general(
                    left, grads[mate, column], down_rows, preferred_element_type=jnp.float32
                )
                total = term if total is None else total + term
            terms.append(total)
        return terms

    def sum_copy(column, kind):
        source = (diag, diag, soon, soon, late, late)[kind].at[column, kind % 2]
        if kind < 2:
            dest = relay.at[column, kind]
        else:
            first = (half, 0, 0, half)[kind - 2]
            dest = summed.at[1 - kind % 2, column, pl.ds(first, half)]
        return pltpu.make_async_remote_copy(
            src_ref=source, dst_ref=dest,
            send_sem=sum_send.at[column, kind], recv_sem=sum_recv.at[column, kind],
            device_id=(adders[(1, 2, 2, 1, 2, 1)[kind]], tens), device_id_type=MESH,
        )

    def sum_onward(column):
        for side in range(2):
            sum_copy(column, side).wait_recv()
            both = late[column, side].astype(jnp.float32) + relay[column, side].astype(jnp.float32)
            late[column, side] = both.astype(late.dtype)
            sum_copy(column, 4 + side).start()

    def sum_complete(column):
        at = pl.ds(column * CHUNK, CHUNK)
        for kind in range(2, 6):
            sum_copy(column, kind).wait_recv()
        total = weight_grad_ref[:, at] + summed[0, column].astype(jnp.float32)
        weight_grad_ref[:, at] = total + summed[1, column].astype(jnp.float32)

    for column in range(columns):
        grad_complete(column)
        at = pl.ds(column * CHUNK, CHUNK)
        for which in (3, 2, 1, 0):
            low_half, high_half = side_term(which, column)
            if which == 3:
                diag[column, 0] = low_half.astype(diag.dtype)
                sum_copy(column, 0).start()
                diag[column, 1] = high_half.astype(diag.dtype)
                sum_copy(column, 1).start()
            elif which == 2:
                soon[column, 0] = high_half.astype(soon.dtype)
                sum_copy(column, 2).start()
                late[column, 0] = low_half.astype(late.dtype)
            elif which == 1:
                soon[column, 1] = low_half.astype(soon.dtype)
                sum_copy(column, 3).start()
                late[column, 1] = high_half.astype(late.dtype)
            else:
                weight_grad_ref[:half, at] = low_half
                weight_grad_ref[half:, at] = high_half
        if column >= 1 and column + 1 < columns:
            grad_onward(column + 1)
        sum_onward(column)
    for column in range(columns):
        sum_complete(column)

    for column in range(columns):
        for kind in range(len(grad_routes)):
            grad_copy(column, kind).wait_send()
        for kind in range(6):
            sum_copy(column, kind).wait_send()


def local(tokens, block_target, doc_lengths, qkv_weight, out_grad):
    peers = lax.axis_size("dp")
    rows, width = tokens.shape
    blocks = rows // BLK
    parts = width // CHUNK
    depth, columns = qkv_weight.shape
    tensors = depth // width
    wide = depth // parts
    pairs = columns // CHUNK
    low = jnp.bfloat16
    dma = pltpu.SemaphoreType.DMA
    vmem = pl.BlockSpec(memory_space=pltpu.VMEM)
    smem = pl.BlockSpec(memory_space=pltpu.SMEM)
    return pl.pallas_call(
        step_kernel,
        out_shape=(
            jax.ShapeDtypeStruct(out_grad.shape, low),
            jax.ShapeDtypeStruct((rows, columns), jnp.float32),
        ),
        in_specs=[smem, smem, vmem, pl.BlockSpec(memory_space=pl.ANY), vmem],
        out_specs=(vmem, vmem),
        scratch_shapes=[
            pltpu.VMEM((8, 128), jnp.int32),
            pltpu.VMEM((peers, 8, 128), jnp.int32),
            pltpu.SMEM((peers, 8, 128), jnp.int32),
            pltpu.VMEM((parts, peers, BLK, CHUNK), low),
            *[pltpu.VMEM((peers, BLK, CHUNK), low) for _ in range(parts)],
            pltpu.VMEM((parts, rows, wide), low),
            pltpu.VMEM((parts, tensors, CHUNK, columns), low),
            pltpu.VMEM((rows, columns), low),
            pltpu.VMEM((parts, rows, 6 * CHUNK), low),
            pltpu.VMEM((4, pairs, rows, CHUNK), low),
            *[pltpu.VMEM((pairs, 2, rows // 2, CHUNK), low) for _ in range(4)],
            pltpu.VMEM((2, pairs, rows, CHUNK), low),
            pltpu.VMEM((rows, rows), low),
            pltpu.VMEM((rows, HD), jnp.float32),
            pltpu.VMEM((rows, HD), jnp.float32),
            dma((peers,)), dma((peers,)),
            dma((parts, peers)), dma((parts, peers)),
            dma((parts, 8)), dma((parts, 8)),
            dma((parts,)), dma,
            dma((parts, 4, 2)), dma((parts, 4, 2)),
            dma((parts, 8)), dma((parts, 8)),
            dma((pairs, 4)), dma((pairs, 4)),
            dma((pairs, 6)), dma((pairs, 6)),
        ],
        compiler_params=pltpu.CompilerParams(
            collective_id=0, has_side_effects=True, vmem_limit_bytes=64 * 2**20
        ),
    )(
        block_target,
        doc_lengths,
        tokens.reshape(blocks, BLK, width),
        qkv_weight.reshape(tensors, parts, CHUNK, columns),
        out_grad,
    )


def solution(mesh):
    placed = (P("dp", "tensor"), P("dp"), P("dp", None), P(None, "tensor"), P("dp", "tensor"))
    return jax.shard_map(
        local,
        mesh=mesh,
        in_specs=placed,
        out_specs=(P("dp", "tensor"), P("dp", "tensor")),
        check_vma=False,
    )
```

```python
import jax
import jax.numpy as jnp
from jax import lax
from jax.experimental import pallas as pl
from jax.experimental.pallas import tpu as pltpu
from jax.sharding import PartitionSpec as P

HD = 128
GQ = 8
BLK = 128
RING = 4
CHUNK = 256
MESH = pl.DeviceIdType.MESH


def peer_at(me, step):
    along_x = (me // RING + step // RING) % RING
    along_z = (me % RING + step % RING) % RING
    return along_x * RING + along_z


def step_kernel(
    target_ref, docs_ref, tok_ref, w_ref, grad_ref, attn_ref, weight_grad_ref,
    tag_out, tags, tags_smem, out_buf, arr0, arr1, arr2, arr3, g, w_buf, qkv,
    mt, grads, diag, soon, late, relay, summed, bias, key_grad, value_grad,
    tag_send, tag_recv, move_send, move_recv, y_send, y_recv, w_sem, smem_sem,
    cross_send, cross_recv, m_send, m_recv, grad_send, grad_recv, sum_send, sum_recv,
):
    arrived = (arr0, arr1, arr2, arr3)
    parts = len(arrived)
    blocks = tok_ref.shape[0]
    peers = tags.shape[0]
    rows = blocks * BLK
    half = rows // 2
    columns = weight_grad_ref.shape[1] // CHUNK
    me = lax.axis_index("dp")
    tens = lax.axis_index("tensor")
    at_x, at_z = me // RING, me % RING
    along_y, core = tens // 2, tens % 2
    up = ((along_y + 1) % RING) * 2 + core
    down = ((along_y + RING - 1) % RING) * 2 + core
    far = ((along_y + 2) % RING) * 2 + core
    twin = along_y * 2 + 1 - core
    near_x = at_x + 1 - 2 * (at_x % 2)
    near_z = at_z + 1 - 2 * (at_z % 2)
    mates = ((at_x, at_z), (near_x, at_z), (at_x, near_z), (near_x, near_z))
    adders = (
        me,
        (RING - 1 - at_x) * RING + at_z,
        at_x * RING + RING - 1 - at_z,
        (RING - 1 - at_x) * RING + RING - 1 - at_z,
    )

    def mate_id(mate):
        return mates[mate][0] * RING + mates[mate][1]

    def lanes(which, width=CHUNK):
        return pl.ds(pl.multiple_of(which * width, width), width)

    def weight_copy(part):
        return pltpu.make_async_copy(w_ref.at[:, part], w_buf.at[part], w_sem.at[part])

    for part in range(parts):
        weight_copy(part).start()

    row_of = lax.broadcasted_iota(jnp.int32, tag_out.shape, 0)
    tile = jnp.zeros(tag_out.shape, jnp.int32)
    for slot in range(blocks):
        tile = jnp.where(row_of == slot, target_ref[slot], tile)
    tag_out[...] = tile

    barrier = pltpu.get_barrier_semaphore()

    @pl.loop(1, peers)
    def _(step):
        pl.semaphore_signal(barrier, inc=1, device_id=(peer_at(me, step), tens), device_id_type=MESH)

    for other in (up, down, twin):
        pl.semaphore_signal(barrier, inc=1, device_id=(me, other), device_id_type=MESH)

    def block_for(peer):
        picked = jnp.int32(0)
        for slot in range(blocks):
            picked = jnp.where(target_ref[slot] // blocks == peer, slot, picked)
        return picked

    def pack(part):
        @pl.loop(0, peers)
        def _(peer):
            out_buf[part, peer] = tok_ref[block_for(peer), :, part * CHUNK : (part + 1) * CHUNK]

    def tag_copy(step):
        return pltpu.make_async_remote_copy(
            src_ref=tag_out, dst_ref=tags.at[me],
            send_sem=tag_send.at[step], recv_sem=tag_recv.at[step],
            device_id=(peer_at(me, step), tens), device_id_type=MESH,
        )

    def move_copy(part, step):
        peer = peer_at(me, step)
        return pltpu.make_async_remote_copy(
            src_ref=out_buf.at[part, peer], dst_ref=arrived[part].at[me],
            send_sem=move_send.at[part, step], recv_sem=move_recv.at[part, step],
            device_id=(peer, tens), device_id_type=MESH,
        )

    def send_part(part):
        @pl.loop(1, peers)
        def _(step):
            move_copy(part, step).start()

        arrived[part][me] = out_buf[part, me]

    pack(0)
    pl.semaphore_wait(barrier, peers - 1 + 3)

    @pl.loop(1, peers)
    def _(step):
        tag_copy(step).start()

    send_part(0)
    for part in range(1, parts):
        pack(part)
        send_part(part)
    tags[me] = tag_out[...]

    query_at = lax.broadcasted_iota(jnp.int32, bias.shape, 0)
    key_at = lax.broadcasted_iota(jnp.int32, bias.shape, 1)
    allowed = key_at <= query_at
    doc_end = jnp.int32(0)
    for doc in range(docs_ref.shape[1]):
        doc_end = doc_end + docs_ref[0, doc]
        allowed = allowed & ((query_at >= doc_end) == (key_at >= doc_end))
    bias[...] = jnp.where(allowed, 0.0, -jnp.inf).astype(bias.dtype)
    key_grad[...] = jnp.zeros_like(key_grad)
    value_grad[...] = jnp.zeros_like(value_grad)

    @pl.loop(1, peers)
    def _(step):
        tag_copy(step).wait()

    to_smem = pltpu.make_async_copy(tags, tags_smem, smem_sem)
    to_smem.start()
    to_smem.wait()

    def source_of(slot):
        def look(peer, found):
            for entry in range(blocks):
                found = jnp.where(tags_smem[peer, entry, 0] == me * blocks + slot, peer, found)
            return found

        return lax.fori_loop(0, peers, look, jnp.int32(0))

    sources = [source_of(slot) for slot in range(blocks)]

    def ring_routes(count):
        return (
            (tens, up, 0, count),
            (tens, down, 0, count),
            (tens, twin, 0, count),
            (down, up, 0, count // 2),
            (down, twin, 0, count),
            (up, down, count // 2, count // 2),
            (up, twin, 0, count),
            (far, twin, 0, count),
        )

    share = rows // 8
    token_routes = ring_routes(rows)
    moved_routes = ring_routes(share)

    def token_hop(part, kind):
        owner, dest, first, count = token_routes[kind]
        piece = g.at[part, pl.ds(first, count), lanes(owner)]
        return pltpu.make_async_remote_copy(
            src_ref=piece, dst_ref=piece,
            send_sem=y_send.at[part, kind], recv_sem=y_recv.at[part, kind],
            device_id=(me, dest), device_id_type=MESH,
        )

    def moved_hop(part, kind):
        owner, dest, first, count = moved_routes[kind]
        at = pl.ds(pl.multiple_of(owner * share + first, 16), count)
        piece = mt.at[part, at, pl.ds(0, 6 * CHUNK)]
        return pltpu.make_async_remote_copy(
            src_ref=piece, dst_ref=piece,
            send_sem=m_send.at[part, kind], recv_sem=m_recv.at[part, kind],
            device_id=(me, dest), device_id_type=MESH,
        )

    def begin(hop, part):
        for kind in (0, 1, 2):
            hop(part, kind).start()

    def onward(hop, part):
        hop(part, 0).wait_recv()
        hop(part, 3).start()
        hop(part, 4).start()
        hop(part, 1).wait_recv()
        hop(part, 5).start()
        hop(part, 6).start()

    def last(hop, part):
        hop(part, 3).wait_recv()
        hop(part, 5).wait_recv()
        hop(part, 7).start()

    def complete(hop, part):
        for kind in (2, 4, 6, 7):
            hop(part, kind).wait_recv()

    def slice_of(device, part, flip):
        along_x, along_z = device
        along_x = RING - 1 - along_x if flip else along_x
        along_z = along_z + (RING - 1 - 2 * along_z) * ((along_z + part // 2) % 2)
        return lanes(along_x * 2 + along_z // 2)

    def cross_rows(part):
        if part < 2:
            return pl.ds(pl.multiple_of(tens * share, share), share)
        return pl.ds(pl.multiple_of(core * half, half), half)

    def cross_copy(part, mate, flip):
        at = cross_rows(part)
        return pltpu.make_async_remote_copy(
            src_ref=g.at[part, at, slice_of(mates[mate], part, flip)],
            dst_ref=mt.at[part, at, pl.ds((2 * mate - 2 + flip) * CHUNK, CHUNK)],
            send_sem=cross_send.at[part, mate, flip], recv_sem=cross_recv.at[part, mate, flip],
            device_id=(mate_id(mate), tens), device_id_type=MESH,
        )

    def twin_copy(part):
        piece = mt.at[part, cross_rows(part)]
        return pltpu.make_async_remote_copy(
            src_ref=piece, dst_ref=piece,
            send_sem=m_send.at[part, 2], recv_sem=m_recv.at[part, 2],
            device_id=(me, twin), device_id_type=MESH,
        )

    def cross_start(part):
        for mate in (1, 2, 3):
            for flip in range(2):
                cross_copy(part, mate, flip).start()

    def moved_begin(part):
        for mate in (1, 2, 3):
            for flip in range(2):
                cross_copy(part, mate, flip).wait_recv()
        if part < 2:
            begin(moved_hop, part)
        else:
            twin_copy(part).start()

    def multiply(part):
        weight_copy(part).wait()

        @pl.loop(0, columns)
        def _(column):
            at = lanes(column)
            weights = w_buf[part, :, :, at].reshape(g.shape[2], CHUNK)
            term = jnp.dot(g[part], weights, preferred_element_type=jnp.float32)
            if part == 0:
                weight_grad_ref[:, at] = term
            elif part < parts - 1:
                weight_grad_ref[:, at] += term
            else:
                qkv[:, at] = (weight_grad_ref[:, at] + term).astype(qkv.dtype)

    for part in range(parts):
        @pl.loop(1, peers)
        def _(step):
            move_copy(part, step).wait_recv()

        for slot in range(blocks):
            g[part, slot * BLK : (slot + 1) * BLK, lanes(tens)] = arrived[part][sources[slot]]
        begin(token_hop, part)
        if part > 0:
            complete(token_hop, part - 1)
            cross_start(part - 1)
            multiply(part - 1)
        onward(token_hop, part)
        if part == 2:
            moved_begin(0)
        if part == 3:
            onward(moved_hop, 0)
            moved_begin(1)
        last(token_hop, part)
    complete(token_hop, parts - 1)
    cross_start(parts - 1)
    multiply(parts - 1)

    factor = HD ** (-0.5)
    key_cols = pl.ds(GQ * HD, HD)
    value_cols = pl.ds((GQ + 1) * HD, HD)
    across = (((1,), (1,)), ((), ()))
    down_rows = (((0,), (0,)), ((), ()))

    def head(pair, which):
        cols = lanes(2 * pair + which, HD)
        for block in range(2):
            at = pl.ds(block * half, half)
            keys = pl.ds(0, (block + 1) * half)
            query = qkv[at, cols]
            key = qkv[keys, key_cols]
            value = qkv[keys, value_cols]
            grad_out = grad_ref[at, cols]
            scores = lax.dot_general(query, key, across, preferred_element_type=jnp.float32)
            scores = scores * factor + bias[at, keys].astype(jnp.float32)
            exponent = jnp.exp(scores - jnp.max(scores, axis=1, keepdims=True))
            prob = exponent * (1.0 / jnp.sum(exponent, axis=1, keepdims=True))
            prob_low = prob.astype(jnp.bfloat16)
            attn_ref[at, cols] = jnp.dot(
                prob_low, value, preferred_element_type=jnp.float32
            ).astype(attn_ref.dtype)
            grad_prob = lax.dot_general(grad_out, value, across, preferred_element_type=jnp.float32)
            row_dot = jnp.sum(prob * grad_prob, axis=1, keepdims=True)
            grad_score = (prob * (grad_prob - row_dot)).astype(jnp.bfloat16)
            grad_query = jnp.dot(grad_score, key, preferred_element_type=jnp.float32) * factor
            grads[0, pair, at, lanes(which, HD)] = grad_query.astype(grads.dtype)
            key_grad[keys, :] += lax.dot_general(
                grad_score, query, down_rows, preferred_element_type=jnp.float32
            )
            value_grad[keys, :] += lax.dot_general(
                prob_low, grad_out, down_rows, preferred_element_type=jnp.float32
            )

    def heads(pair):
        for which in range(2):
            head(pair, which)

    grad_routes = ((0, 1, 1, 0, rows), (0, 2, 2, 0, rows), (1, 2, 3, 0, half), (2, 1, 3, half, half))

    def grad_copy(pair, kind):
        source, mate, slot, first, count = grad_routes[kind]
        return pltpu.make_async_remote_copy(
            src_ref=grads.at[source, pair, pl.ds(first, count)],
            dst_ref=grads.at[slot, pair, pl.ds(first, count)],
            send_sem=grad_send.at[pair, kind], recv_sem=grad_recv.at[pair, kind],
            device_id=(mate_id(mate), tens), device_id_type=MESH,
        )

    def grad_begin(pair):
        grad_copy(pair, 0).start()
        grad_copy(pair, 1).start()

    def grad_onward(pair):
        grad_copy(pair, 0).wait_recv()
        grad_copy(pair, 2).start()
        grad_copy(pair, 1).wait_recv()
        grad_copy(pair, 3).start()

    def grad_complete(pair):
        grad_copy(pair, 2).wait_recv()
        grad_copy(pair, 3).wait_recv()

    heads(0)
    grad_begin(0)
    last(moved_hop, 0)
    onward(moved_hop, 1)
    moved_begin(2)
    heads(1)
    grad_begin(1)
    last(moved_hop, 1)
    moved_begin(3)
    heads(2)
    grad_begin(2)
    grad_onward(0)
    heads(3)
    grad_begin(3)
    grads[0, GQ // 2, :, :HD] = (key_grad[...] * factor).astype(grads.dtype)
    grads[0, GQ // 2, :, HD:] = value_grad[...].astype(grads.dtype)
    grad_begin(4)
    grad_onward(1)

    for part in range(parts):
        for kind in range(8):
            token_hop(part, kind).wait_send()
        if part < 2:
            complete(moved_hop, part)
            for kind in range(8):
                moved_hop(part, kind).wait_send()
        else:
            twin_copy(part).wait()
        for mate in (1, 2, 3):
            for flip in range(2):
                cross_copy(part, mate, flip).wait_send()

        @pl.loop(1, peers)
        def _(step):
            move_copy(part, step).wait_send()

    def side_term(which, column):
        parity = (at_z + which // 2) % 2
        terms = []
        for side in range(2):
            total = None
            for mate in range(4):
                if mate == 0:
                    along_z = at_z if which < 2 else RING - 1 - at_z
                    along_x = at_x if which % 2 == 0 else RING - 1 - at_x
                    left = g[2 * parity + side, :, lanes(along_x * 2 + along_z // 2)]
                else:
                    left = mt[2 * parity + side, :, pl.ds((2 * mate - 2 + which % 2) * CHUNK, CHUNK)]
                term = lax.dot_general(
                    left, grads[mate, column], down_rows, preferred_element_type=jnp.float32
                )
                total = term if total is None else total + term
            terms.append(total)
        return terms

    def sum_copy(column, kind):
        source = (diag, diag, soon, soon, late, late)[kind].at[column, kind % 2]
        if kind < 2:
            dest = relay.at[column, kind]
        else:
            first = (half, 0, 0, half)[kind - 2]
            dest = summed.at[1 - kind % 2, column, pl.ds(first, half)]
        return pltpu.make_async_remote_copy(
            src_ref=source, dst_ref=dest,
            send_sem=sum_send.at[column, kind], recv_sem=sum_recv.at[column, kind],
            device_id=(adders[(1, 2, 2, 1, 2, 1)[kind]], tens), device_id_type=MESH,
        )

    def sum_onward(column):
        for side in range(2):
            sum_copy(column, side).wait_recv()
            both = late[column, side].astype(jnp.float32) + relay[column, side].astype(jnp.float32)
            late[column, side] = both.astype(late.dtype)
            sum_copy(column, 4 + side).start()

    def sum_complete(column):
        at = pl.ds(column * CHUNK, CHUNK)
        for kind in range(2, 6):
            sum_copy(column, kind).wait_recv()
        total = weight_grad_ref[:, at] + summed[0, column].astype(jnp.float32)
        weight_grad_ref[:, at] = total + summed[1, column].astype(jnp.float32)

    for column in range(columns):
        grad_complete(column)
        at = pl.ds(column * CHUNK, CHUNK)
        for which in (3, 2, 1, 0):
            low_half, high_half = side_term(which, column)
            if which == 3:
                diag[column, 0] = low_half.astype(diag.dtype)
                sum_copy(column, 0).start()
                diag[column, 1] = high_half.astype(diag.dtype)
                sum_copy(column, 1).start()
            elif which == 2:
                soon[column, 0] = high_half.astype(soon.dtype)
                sum_copy(column, 2).start()
                late[column, 0] = low_half.astype(late.dtype)
            elif which == 1:
                soon[column, 1] = low_half.astype(soon.dtype)
                sum_copy(column, 3).start()
                late[column, 1] = high_half.astype(late.dtype)
            else:
                weight_grad_ref[:half, at] = low_half
                weight_grad_ref[half:, at] = high_half
        if column >= 1 and column + 1 < columns:
            grad_onward(column + 1)
        sum_onward(column)
    for column in range(columns):
        sum_complete(column)

    for column in range(columns):
        for kind in range(len(grad_routes)):
            grad_copy(column, kind).wait_send()
        for kind in range(6):
            sum_copy(column, kind).wait_send()


def local(tokens, block_target, doc_lengths, qkv_weight, out_grad):
    peers = lax.axis_size("dp")
    rows, width = tokens.shape
    blocks = rows // BLK
    parts = width // CHUNK
    depth, columns = qkv_weight.shape
    tensors = depth // width
    wide = depth // parts
    pairs = columns // CHUNK
    low = jnp.bfloat16
    dma = pltpu.SemaphoreType.DMA
    vmem = pl.BlockSpec(memory_space=pltpu.VMEM)
    smem = pl.BlockSpec(memory_space=pltpu.SMEM)
    return pl.pallas_call(
        step_kernel,
        out_shape=(
            jax.ShapeDtypeStruct(out_grad.shape, low),
            jax.ShapeDtypeStruct((rows, columns), jnp.float32),
        ),
        in_specs=[smem, smem, vmem, pl.BlockSpec(memory_space=pl.ANY), vmem],
        out_specs=(vmem, vmem),
        scratch_shapes=[
            pltpu.VMEM((8, 128), jnp.int32),
            pltpu.VMEM((peers, 8, 128), jnp.int32),
            pltpu.SMEM((peers, 8, 128), jnp.int32),
            pltpu.VMEM((parts, peers, BLK, CHUNK), low),
            *[pltpu.VMEM((peers, BLK, CHUNK), low) for _ in range(parts)],
            pltpu.VMEM((parts, rows, wide), low),
            pltpu.VMEM((parts, tensors, CHUNK, columns), low),
            pltpu.VMEM((rows, columns), low),
            pltpu.VMEM((parts, rows, 6 * CHUNK), low),
            pltpu.VMEM((4, pairs, rows, CHUNK), low),
            *[pltpu.VMEM((pairs, 2, rows // 2, CHUNK), low) for _ in range(4)],
            pltpu.VMEM((2, pairs, rows, CHUNK), low),
            pltpu.VMEM((rows, rows), low),
            pltpu.VMEM((rows, HD), jnp.float32),
            pltpu.VMEM((rows, HD), jnp.float32),
            dma((peers,)), dma((peers,)),
            dma((parts, peers)), dma((parts, peers)),
            dma((parts, 8)), dma((parts, 8)),
            dma((parts,)), dma,
            dma((parts, 4, 2)), dma((parts, 4, 2)),
            dma((parts, 8)), dma((parts, 8)),
            dma((pairs, 4)), dma((pairs, 4)),
            dma((pairs, 6)), dma((pairs, 6)),
        ],
        compiler_params=pltpu.CompilerParams(
            collective_id=0, has_side_effects=True, vmem_limit_bytes=64 * 2**20
        ),
    )(
        block_target,
        doc_lengths,
        tokens.reshape(blocks, BLK, width),
        qkv_weight.reshape(tensors, parts, CHUNK, columns),
        out_grad,
    )


def solution(mesh):
    placed = (P("dp", "tensor"), P("dp"), P("dp", None), P(None, "tensor"), P("dp", "tensor"))
    return jax.shard_map(
        local,
        mesh=mesh,
        in_specs=placed,
        out_specs=(P("dp", "tensor"), P("dp", "tensor")),
        check_vma=False,
    )
```

```python
import jax
import jax.numpy as jnp
from jax import lax
from jax.experimental import pallas as pl
from jax.experimental.pallas import tpu as pltpu
from jax.sharding import PartitionSpec as P

HD = 128
GQ = 8
BLK = 128
RING = 4
CHUNK = 256
MESH = pl.DeviceIdType.MESH


def peer_at(me, step):
    along_x = (me // RING + step // RING) % RING
    along_z = (me % RING + step % RING) % RING
    return along_x * RING + along_z


def step_kernel(
    target_ref, docs_ref, tok_ref, w_ref, grad_ref, attn_ref, weight_grad_ref,
    tag_out, tags, tags_smem, out_buf, arr0, arr1, arr2, arr3, g, w_buf, qkv,
    mt, grads, diag, soon, late, relay, summed, bias, key_grad, value_grad,
    tag_send, tag_recv, move_send, move_recv, y_send, y_recv, w_sem, smem_sem,
    cross_send, cross_recv, m_send, m_recv, grad_send, grad_recv, sum_send, sum_recv,
):
    arrived = (arr0, arr1, arr2, arr3)
    parts = len(arrived)
    blocks = tok_ref.shape[0]
    peers = tags.shape[0]
    rows = blocks * BLK
    half = rows // 2
    columns = weight_grad_ref.shape[1] // CHUNK
    me = lax.axis_index("dp")
    tens = lax.axis_index("tensor")
    at_x, at_z = me // RING, me % RING
    along_y, core = tens // 2, tens % 2
    up = ((along_y + 1) % RING) * 2 + core
    down = ((along_y + RING - 1) % RING) * 2 + core
    far = ((along_y + 2) % RING) * 2 + core
    twin = along_y * 2 + 1 - core
    near_x = at_x + 1 - 2 * (at_x % 2)
    near_z = at_z + 1 - 2 * (at_z % 2)
    mates = ((at_x, at_z), (near_x, at_z), (at_x, near_z), (near_x, near_z))
    adders = (
        me,
        (RING - 1 - at_x) * RING + at_z,
        at_x * RING + RING - 1 - at_z,
        (RING - 1 - at_x) * RING + RING - 1 - at_z,
    )

    def mate_id(mate):
        return mates[mate][0] * RING + mates[mate][1]

    def lanes(which, width=CHUNK):
        return pl.ds(pl.multiple_of(which * width, width), width)

    def weight_copy(part):
        return pltpu.make_async_copy(w_ref.at[:, part], w_buf.at[part], w_sem.at[part])

    for part in range(parts):
        weight_copy(part).start()

    row_of = lax.broadcasted_iota(jnp.int32, tag_out.shape, 0)
    tile = jnp.zeros(tag_out.shape, jnp.int32)
    for slot in range(blocks):
        tile = jnp.where(row_of == slot, target_ref[slot], tile)
    tag_out[...] = tile

    barrier = pltpu.get_barrier_semaphore()

    @pl.loop(1, peers)
    def _(step):
        pl.semaphore_signal(barrier, inc=1, device_id=(peer_at(me, step), tens), device_id_type=MESH)

    for other in (up, down, twin):
        pl.semaphore_signal(barrier, inc=1, device_id=(me, other), device_id_type=MESH)

    def block_for(peer):
        picked = jnp.int32(0)
        for slot in range(blocks):
            picked = jnp.where(target_ref[slot] // blocks == peer, slot, picked)
        return picked

    def pack(part):
        @pl.loop(0, peers)
        def _(peer):
            out_buf[part, peer] = tok_ref[block_for(peer), :, part * CHUNK : (part + 1) * CHUNK]

    def tag_copy(step):
        return pltpu.make_async_remote_copy(
            src_ref=tag_out, dst_ref=tags.at[me],
            send_sem=tag_send.at[step], recv_sem=tag_recv.at[step],
            device_id=(peer_at(me, step), tens), device_id_type=MESH,
        )

    def move_copy(part, step):
        peer = peer_at(me, step)
        return pltpu.make_async_remote_copy(
            src_ref=out_buf.at[part, peer], dst_ref=arrived[part].at[me],
            send_sem=move_send.at[part, step], recv_sem=move_recv.at[part, step],
            device_id=(peer, tens), device_id_type=MESH,
        )

    def send_part(part):
        @pl.loop(1, peers)
        def _(step):
            move_copy(part, step).start()

        arrived[part][me] = out_buf[part, me]

    pack(0)
    pl.semaphore_wait(barrier, peers - 1 + 3)

    @pl.loop(1, peers)
    def _(step):
        tag_copy(step).start()

    send_part(0)
    for part in range(1, parts):
        pack(part)
        send_part(part)
    tags[me] = tag_out[...]

    query_at = lax.broadcasted_iota(jnp.int32, bias.shape, 0)
    key_at = lax.broadcasted_iota(jnp.int32, bias.shape, 1)
    allowed = key_at <= query_at
    doc_end = jnp.int32(0)
    for doc in range(docs_ref.shape[1]):
        doc_end = doc_end + docs_ref[0, doc]
        allowed = allowed & ((query_at >= doc_end) == (key_at >= doc_end))
    bias[...] = jnp.where(allowed, 0.0, -jnp.inf).astype(bias.dtype)
    key_grad[...] = jnp.zeros_like(key_grad)
    value_grad[...] = jnp.zeros_like(value_grad)

    @pl.loop(1, peers)
    def _(step):
        tag_copy(step).wait()

    to_smem = pltpu.make_async_copy(tags, tags_smem, smem_sem)
    to_smem.start()
    to_smem.wait()

    def source_of(slot):
        def look(peer, found):
            for entry in range(blocks):
                found = jnp.where(tags_smem[peer, entry, 0] == me * blocks + slot, peer, found)
            return found

        return lax.fori_loop(0, peers, look, jnp.int32(0))

    sources = [source_of(slot) for slot in range(blocks)]

    def ring_routes(count):
        return (
            (tens, up, 0, count),
            (tens, down, 0, count),
            (tens, twin, 0, count),
            (down, up, 0, count // 2),
            (down, twin, 0, count),
            (up, down, count // 2, count // 2),
            (up, twin, 0, count),
            (far, twin, 0, count),
        )

    share = rows // 8
    token_routes = ring_routes(rows)
    moved_routes = ring_routes(share)

    def token_hop(part, kind):
        owner, dest, first, count = token_routes[kind]
        piece = g.at[part, pl.ds(first, count), lanes(owner)]
        return pltpu.make_async_remote_copy(
            src_ref=piece, dst_ref=piece,
            send_sem=y_send.at[part, kind], recv_sem=y_recv.at[part, kind],
            device_id=(me, dest), device_id_type=MESH,
        )

    def moved_hop(part, kind):
        owner, dest, first, count = moved_routes[kind]
        at = pl.ds(pl.multiple_of(owner * share + first, 16), count)
        piece = mt.at[part, at, pl.ds(0, 6 * CHUNK)]
        return pltpu.make_async_remote_copy(
            src_ref=piece, dst_ref=piece,
            send_sem=m_send.at[part, kind], recv_sem=m_recv.at[part, kind],
            device_id=(me, dest), device_id_type=MESH,
        )

    def begin(hop, part):
        for kind in (0, 1, 2):
            hop(part, kind).start()

    def onward(hop, part):
        hop(part, 0).wait_recv()
        hop(part, 3).start()
        hop(part, 4).start()
        hop(part, 1).wait_recv()
        hop(part, 5).start()
        hop(part, 6).start()

    def last(hop, part):
        hop(part, 3).wait_recv()
        hop(part, 5).wait_recv()
        hop(part, 7).start()

    def complete(hop, part):
        for kind in (2, 4, 6, 7):
            hop(part, kind).wait_recv()

    def slice_of(device, part, flip):
        along_x, along_z = device
        along_x = RING - 1 - along_x if flip else along_x
        along_z = along_z + (RING - 1 - 2 * along_z) * ((along_z + part // 2) % 2)
        return lanes(along_x * 2 + along_z // 2)

    def cross_rows(part):
        if part < 2:
            return pl.ds(pl.multiple_of(tens * share, share), share)
        return pl.ds(pl.multiple_of(core * half, half), half)

    def cross_copy(part, mate, flip):
        at = cross_rows(part)
        return pltpu.make_async_remote_copy(
            src_ref=g.at[part, at, slice_of(mates[mate], part, flip)],
            dst_ref=mt.at[part, at, pl.ds((2 * mate - 2 + flip) * CHUNK, CHUNK)],
            send_sem=cross_send.at[part, mate, flip], recv_sem=cross_recv.at[part, mate, flip],
            device_id=(mate_id(mate), tens), device_id_type=MESH,
        )

    def twin_copy(part):
        piece = mt.at[part, cross_rows(part)]
        return pltpu.make_async_remote_copy(
            src_ref=piece, dst_ref=piece,
            send_sem=m_send.at[part, 2], recv_sem=m_recv.at[part, 2],
            device_id=(me, twin), device_id_type=MESH,
        )

    def cross_start(part):
        for mate in (1, 2, 3):
            for flip in range(2):
                cross_copy(part, mate, flip).start()

    def moved_begin(part):
        for mate in (1, 2, 3):
            for flip in range(2):
                cross_copy(part, mate, flip).wait_recv()
        if part < 2:
            begin(moved_hop, part)
        else:
            twin_copy(part).start()

    def multiply(part):
        weight_copy(part).wait()

        @pl.loop(0, columns)
        def _(column):
            at = lanes(column)
            weights = w_buf[part, :, :, at].reshape(g.shape[2], CHUNK)
            term = jnp.dot(g[part], weights, preferred_element_type=jnp.float32)
            if part == 0:
                weight_grad_ref[:, at] = term
            elif part < parts - 1:
                weight_grad_ref[:, at] += term
            else:
                qkv[:, at] = (weight_grad_ref[:, at] + term).astype(qkv.dtype)

    for part in range(parts):
        @pl.loop(1, peers)
        def _(step):
            move_copy(part, step).wait_recv()

        for slot in range(blocks):
            g[part, slot * BLK : (slot + 1) * BLK, lanes(tens)] = arrived[part][sources[slot]]
        begin(token_hop, part)
        if part > 0:
            last(token_hop, part - 1)
            complete(token_hop, part - 1)
            cross_start(part - 1)
            multiply(part - 1)
        onward(token_hop, part)
        if part == 2:
            moved_begin(0)
        if part == 3:
            onward(moved_hop, 0)
            moved_begin(1)
    last(token_hop, parts - 1)
    complete(token_hop, parts - 1)
    cross_start(parts - 1)
    multiply(parts - 1)

    factor = HD ** (-0.5)
    key_cols = pl.ds(GQ * HD, HD)
    value_cols = pl.ds((GQ + 1) * HD, HD)
    across = (((1,), (1,)), ((), ()))
    down_rows = (((0,), (0,)), ((), ()))

    def head(pair, which):
        cols = lanes(2 * pair + which, HD)
        for block in range(2):
            at = pl.ds(block * half, half)
            keys = pl.ds(0, (block + 1) * half)
            query = qkv[at, cols]
            key = qkv[keys, key_cols]
            value = qkv[keys, value_cols]
            grad_out = grad_ref[at, cols]
            scores = lax.dot_general(query, key, across, preferred_element_type=jnp.float32)
            scores = scores * factor + bias[at, keys].astype(jnp.float32)
            exponent = jnp.exp(scores - jnp.max(scores, axis=1, keepdims=True))
            prob = exponent * (1.0 / jnp.sum(exponent, axis=1, keepdims=True))
            prob_low = prob.astype(jnp.bfloat16)
            attn_ref[at, cols] = jnp.dot(
                prob_low, value, preferred_element_type=jnp.float32
            ).astype(attn_ref.dtype)
            grad_prob = lax.dot_general(grad_out, value, across, preferred_element_type=jnp.float32)
            row_dot = jnp.sum(prob * grad_prob, axis=1, keepdims=True)
            grad_score = (prob * (grad_prob - row_dot)).astype(jnp.bfloat16)
            grad_query = jnp.dot(grad_score, key, preferred_element_type=jnp.float32) * factor
            grads[0, pair, at, lanes(which, HD)] = grad_query.astype(grads.dtype)
            key_grad[keys, :] += lax.dot_general(
                grad_score, query, down_rows, preferred_element_type=jnp.float32
            )
            value_grad[keys, :] += lax.dot_general(
                prob_low, grad_out, down_rows, preferred_element_type=jnp.float32
            )

    def heads(pair):
        for which in range(2):
            head(pair, which)

    grad_routes = ((0, 1, 1, 0, rows), (0, 2, 2, 0, rows), (1, 2, 3, 0, half), (2, 1, 3, half, half))

    def grad_copy(pair, kind):
        source, mate, slot, first, count = grad_routes[kind]
        return pltpu.make_async_remote_copy(
            src_ref=grads.at[source, pair, pl.ds(first, count)],
            dst_ref=grads.at[slot, pair, pl.ds(first, count)],
            send_sem=grad_send.at[pair, kind], recv_sem=grad_recv.at[pair, kind],
            device_id=(mate_id(mate), tens), device_id_type=MESH,
        )

    def grad_begin(pair):
        grad_copy(pair, 0).start()
        grad_copy(pair, 1).start()

    def grad_onward(pair):
        grad_copy(pair, 0).wait_recv()
        grad_copy(pair, 2).start()
        grad_copy(pair, 1).wait_recv()
        grad_copy(pair, 3).start()

    def grad_complete(pair):
        grad_copy(pair, 2).wait_recv()
        grad_copy(pair, 3).wait_recv()

    heads(0)
    grad_begin(0)
    last(moved_hop, 0)
    onward(moved_hop, 1)
    moved_begin(2)
    heads(1)
    grad_begin(1)
    last(moved_hop, 1)
    moved_begin(3)
    heads(2)
    grad_begin(2)
    grad_onward(0)
    heads(3)
    grad_begin(3)
    grads[0, GQ // 2, :, :HD] = (key_grad[...] * factor).astype(grads.dtype)
    grads[0, GQ // 2, :, HD:] = value_grad[...].astype(grads.dtype)
    grad_begin(4)

    for part in range(parts):
        for kind in range(8):
            token_hop(part, kind).wait_send()
        if part < 2:
            complete(moved_hop, part)
            for kind in range(8):
                moved_hop(part, kind).wait_send()
        else:
            twin_copy(part).wait()
        for mate in (1, 2, 3):
            for flip in range(2):
                cross_copy(part, mate, flip).wait_send()

        @pl.loop(1, peers)
        def _(step):
            move_copy(part, step).wait_send()

    def side_term(which, column):
        parity = (at_z + which // 2) % 2
        terms = []
        for side in range(2):
            total = None
            for mate in range(4):
                if mate == 0:
                    along_z = at_z if which < 2 else RING - 1 - at_z
                    along_x = at_x if which % 2 == 0 else RING - 1 - at_x
                    left = g[2 * parity + side, :, lanes(along_x * 2 + along_z // 2)]
                else:
                    left = mt[2 * parity + side, :, pl.ds((2 * mate - 2 + which % 2) * CHUNK, CHUNK)]
                term = lax.dot_general(
                    left, grads[mate, column], down_rows, preferred_element_type=jnp.float32
                )
                total = term if total is None else total + term
            terms.append(total)
        return terms

    def sum_copy(column, kind):
        source = (diag, diag, soon, soon, late, late)[kind].at[column, kind % 2]
        if kind < 2:
            dest = relay.at[column, kind]
        else:
            first = (half, 0, 0, half)[kind - 2]
            dest = summed.at[1 - kind % 2, column, pl.ds(first, half)]
        return pltpu.make_async_remote_copy(
            src_ref=source, dst_ref=dest,
            send_sem=sum_send.at[column, kind], recv_sem=sum_recv.at[column, kind],
            device_id=(adders[(1, 2, 2, 1, 2, 1)[kind]], tens), device_id_type=MESH,
        )

    def sum_onward(column):
        for side in range(2):
            sum_copy(column, side).wait_recv()
            both = late[column, side].astype(jnp.float32) + relay[column, side].astype(jnp.float32)
            late[column, side] = both.astype(late.dtype)
            sum_copy(column, 4 + side).start()

    def sum_complete(column):
        at = pl.ds(column * CHUNK, CHUNK)
        for kind in range(2, 6):
            sum_copy(column, kind).wait_recv()
        total = weight_grad_ref[:, at] + summed[0, column].astype(jnp.float32)
        weight_grad_ref[:, at] = total + summed[1, column].astype(jnp.float32)

    for column in range(columns):
        grad_complete(column)
        at = pl.ds(column * CHUNK, CHUNK)
        for which in (3, 2, 1, 0):
            low_half, high_half = side_term(which, column)
            if which == 3:
                diag[column, 0] = low_half.astype(diag.dtype)
                sum_copy(column, 0).start()
                diag[column, 1] = high_half.astype(diag.dtype)
                sum_copy(column, 1).start()
            elif which == 2:
                soon[column, 0] = high_half.astype(soon.dtype)
                sum_copy(column, 2).start()
                late[column, 0] = low_half.astype(late.dtype)
            elif which == 1:
                soon[column, 1] = low_half.astype(soon.dtype)
                sum_copy(column, 3).start()
                late[column, 1] = high_half.astype(late.dtype)
            else:
                weight_grad_ref[:half, at] = low_half
                weight_grad_ref[half:, at] = high_half
        if column + 1 < columns:
            grad_onward(column + 1)
        sum_onward(column)
        if column >= 2:
            sum_complete(column - 2)
    for column in (columns - 2, columns - 1):
        sum_complete(column)

    for column in range(columns):
        for kind in range(len(grad_routes)):
            grad_copy(column, kind).wait_send()
        for kind in range(6):
            sum_copy(column, kind).wait_send()


def local(tokens, block_target, doc_lengths, qkv_weight, out_grad):
    peers = lax.axis_size("dp")
    rows, width = tokens.shape
    blocks = rows // BLK
    parts = width // CHUNK
    depth, columns = qkv_weight.shape
    tensors = depth // width
    wide = depth // parts
    pairs = columns // CHUNK
    low = jnp.bfloat16
    dma = pltpu.SemaphoreType.DMA
    vmem = pl.BlockSpec(memory_space=pltpu.VMEM)
    smem = pl.BlockSpec(memory_space=pltpu.SMEM)
    return pl.pallas_call(
        step_kernel,
        out_shape=(
            jax.ShapeDtypeStruct(out_grad.shape, low),
            jax.ShapeDtypeStruct((rows, columns), jnp.float32),
        ),
        in_specs=[smem, smem, vmem, pl.BlockSpec(memory_space=pl.ANY), vmem],
        out_specs=(vmem, vmem),
        scratch_shapes=[
            pltpu.VMEM((8, 128), jnp.int32),
            pltpu.VMEM((peers, 8, 128), jnp.int32),
            pltpu.SMEM((peers, 8, 128), jnp.int32),
            pltpu.VMEM((parts, peers, BLK, CHUNK), low),
            *[pltpu.VMEM((peers, BLK, CHUNK), low) for _ in range(parts)],
            pltpu.VMEM((parts, rows, wide), low),
            pltpu.VMEM((parts, tensors, CHUNK, columns), low),
            pltpu.VMEM((rows, columns), low),
            pltpu.VMEM((parts, rows, 6 * CHUNK), low),
            pltpu.VMEM((4, pairs, rows, CHUNK), low),
            *[pltpu.VMEM((pairs, 2, rows // 2, CHUNK), low) for _ in range(4)],
            pltpu.VMEM((2, pairs, rows, CHUNK), low),
            pltpu.VMEM((rows, rows), low),
            pltpu.VMEM((rows, HD), jnp.float32),
            pltpu.VMEM((rows, HD), jnp.float32),
            dma((peers,)), dma((peers,)),
            dma((parts, peers)), dma((parts, peers)),
            dma((parts, 8)), dma((parts, 8)),
            dma((parts,)), dma,
            dma((parts, 4, 2)), dma((parts, 4, 2)),
            dma((parts, 8)), dma((parts, 8)),
            dma((pairs, 4)), dma((pairs, 4)),
            dma((pairs, 6)), dma((pairs, 6)),
        ],
        compiler_params=pltpu.CompilerParams(
            collective_id=0, has_side_effects=True, vmem_limit_bytes=64 * 2**20
        ),
    )(
        block_target,
        doc_lengths,
        tokens.reshape(blocks, BLK, width),
        qkv_weight.reshape(tensors, parts, CHUNK, columns),
        out_grad,
    )


def solution(mesh):
    placed = (P("dp", "tensor"), P("dp"), P("dp", None), P(None, "tensor"), P("dp", "tensor"))
    return jax.shard_map(
        local,
        mesh=mesh,
        in_specs=placed,
        out_specs=(P("dp", "tensor"), P("dp", "tensor")),
        check_vma=False,
    )
```

```python
import jax
import jax.numpy as jnp
from jax import lax
from jax.experimental import pallas as pl
from jax.experimental.pallas import tpu as pltpu
from jax.sharding import PartitionSpec as P

HD = 128
GQ = 8
BLK = 128
RING = 4
CHUNK = 256
MESH = pl.DeviceIdType.MESH


def peer_at(me, step):
    along_x = (me // RING + step // RING) % RING
    along_z = (me % RING + step % RING) % RING
    return along_x * RING + along_z


def step_kernel(
    target_ref, docs_ref, tok_ref, w_ref, grad_ref, attn_ref, weight_grad_ref,
    tag_out, tags, tags_smem, out_buf, arr0, arr1, arr2, arr3, g, w_buf, qkv,
    mt, grads, diag, soon, late, relay, summed, bias, key_grad, value_grad,
    tag_send, tag_recv, move_send, move_recv, y_send, y_recv, w_sem, smem_sem,
    cross_send, cross_recv, m_send, m_recv, grad_send, grad_recv, sum_send, sum_recv,
):
    arrived = (arr0, arr1, arr2, arr3)
    parts = len(arrived)
    blocks = tok_ref.shape[0]
    peers = tags.shape[0]
    rows = blocks * BLK
    half = rows // 2
    columns = weight_grad_ref.shape[1] // CHUNK
    me = lax.axis_index("dp")
    tens = lax.axis_index("tensor")
    at_x, at_z = me // RING, me % RING
    along_y, core = tens // 2, tens % 2
    up = ((along_y + 1) % RING) * 2 + core
    down = ((along_y + RING - 1) % RING) * 2 + core
    far = ((along_y + 2) % RING) * 2 + core
    twin = along_y * 2 + 1 - core
    near_x = at_x + 1 - 2 * (at_x % 2)
    near_z = at_z + 1 - 2 * (at_z % 2)
    mates = ((at_x, at_z), (near_x, at_z), (at_x, near_z), (near_x, near_z))
    adders = (
        me,
        (RING - 1 - at_x) * RING + at_z,
        at_x * RING + RING - 1 - at_z,
        (RING - 1 - at_x) * RING + RING - 1 - at_z,
    )

    def mate_id(mate):
        return mates[mate][0] * RING + mates[mate][1]

    def lanes(which, width=CHUNK):
        return pl.ds(pl.multiple_of(which * width, width), width)

    def weight_copy(part):
        return pltpu.make_async_copy(w_ref.at[:, part], w_buf.at[part], w_sem.at[part])

    for part in range(parts):
        weight_copy(part).start()

    row_of = lax.broadcasted_iota(jnp.int32, tag_out.shape, 0)
    tile = jnp.zeros(tag_out.shape, jnp.int32)
    for slot in range(blocks):
        tile = jnp.where(row_of == slot, target_ref[slot], tile)
    tag_out[...] = tile

    barrier = pltpu.get_barrier_semaphore()

    @pl.loop(1, peers)
    def _(step):
        pl.semaphore_signal(barrier, inc=1, device_id=(peer_at(me, step), tens), device_id_type=MESH)

    for other in (up, down, twin):
        pl.semaphore_signal(barrier, inc=1, device_id=(me, other), device_id_type=MESH)

    def block_for(peer):
        picked = jnp.int32(0)
        for slot in range(blocks):
            picked = jnp.where(target_ref[slot] // blocks == peer, slot, picked)
        return picked

    def pack(part):
        @pl.loop(0, peers)
        def _(peer):
            out_buf[part, peer] = tok_ref[block_for(peer), :, part * CHUNK : (part + 1) * CHUNK]

    def tag_copy(step):
        return pltpu.make_async_remote_copy(
            src_ref=tag_out, dst_ref=tags.at[me],
            send_sem=tag_send.at[step], recv_sem=tag_recv.at[step],
            device_id=(peer_at(me, step), tens), device_id_type=MESH,
        )

    def move_copy(part, step):
        peer = peer_at(me, step)
        return pltpu.make_async_remote_copy(
            src_ref=out_buf.at[part, peer], dst_ref=arrived[part].at[me],
            send_sem=move_send.at[part, step], recv_sem=move_recv.at[part, step],
            device_id=(peer, tens), device_id_type=MESH,
        )

    def send_part(part):
        @pl.loop(1, peers)
        def _(step):
            move_copy(part, step).start()

        arrived[part][me] = out_buf[part, me]

    pack(0)
    pl.semaphore_wait(barrier, peers - 1 + 3)

    @pl.loop(1, peers)
    def _(step):
        tag_copy(step).start()

    send_part(0)
    for part in range(1, parts):
        pack(part)
        send_part(part)
    tags[me] = tag_out[...]

    query_at = lax.broadcasted_iota(jnp.int32, bias.shape, 0)
    key_at = lax.broadcasted_iota(jnp.int32, bias.shape, 1)
    allowed = key_at <= query_at
    doc_end = jnp.int32(0)
    for doc in range(docs_ref.shape[1]):
        doc_end = doc_end + docs_ref[0, doc]
        allowed = allowed & ((query_at >= doc_end) == (key_at >= doc_end))
    bias[...] = jnp.where(allowed, 0.0, -jnp.inf).astype(bias.dtype)
    key_grad[...] = jnp.zeros_like(key_grad)
    value_grad[...] = jnp.zeros_like(value_grad)

    @pl.loop(1, peers)
    def _(step):
        tag_copy(step).wait()

    to_smem = pltpu.make_async_copy(tags, tags_smem, smem_sem)
    to_smem.start()
    to_smem.wait()

    def source_of(slot):
        def look(peer, found):
            for entry in range(blocks):
                found = jnp.where(tags_smem[peer, entry, 0] == me * blocks + slot, peer, found)
            return found

        return lax.fori_loop(0, peers, look, jnp.int32(0))

    sources = [source_of(slot) for slot in range(blocks)]

    def ring_routes(count):
        return (
            (tens, up, 0, count),
            (tens, down, 0, count),
            (tens, twin, 0, count),
            (down, up, 0, count // 2),
            (down, twin, 0, count),
            (up, down, count // 2, count // 2),
            (up, twin, 0, count),
            (far, twin, 0, count),
        )

    share = rows // 8
    token_routes = ring_routes(rows)
    moved_routes = ring_routes(share)

    def token_hop(part, kind):
        owner, dest, first, count = token_routes[kind]
        piece = g.at[part, pl.ds(first, count), lanes(owner)]
        return pltpu.make_async_remote_copy(
            src_ref=piece, dst_ref=piece,
            send_sem=y_send.at[part, kind], recv_sem=y_recv.at[part, kind],
            device_id=(me, dest), device_id_type=MESH,
        )

    def moved_hop(part, kind):
        owner, dest, first, count = moved_routes[kind]
        at = pl.ds(pl.multiple_of(owner * share + first, 16), count)
        piece = mt.at[part, at, pl.ds(0, 6 * CHUNK)]
        return pltpu.make_async_remote_copy(
            src_ref=piece, dst_ref=piece,
            send_sem=m_send.at[part, kind], recv_sem=m_recv.at[part, kind],
            device_id=(me, dest), device_id_type=MESH,
        )

    def begin(hop, part):
        for kind in (0, 1, 2):
            hop(part, kind).start()

    def onward(hop, part):
        hop(part, 0).wait_recv()
        hop(part, 3).start()
        hop(part, 4).start()
        hop(part, 1).wait_recv()
        hop(part, 5).start()
        hop(part, 6).start()

    def last(hop, part):
        hop(part, 3).wait_recv()
        hop(part, 5).wait_recv()
        hop(part, 7).start()

    def complete(hop, part):
        for kind in (2, 4, 6, 7):
            hop(part, kind).wait_recv()

    def slice_of(device, part, flip):
        along_x, along_z = device
        along_x = RING - 1 - along_x if flip else along_x
        along_z = along_z + (RING - 1 - 2 * along_z) * ((along_z + part // 2) % 2)
        return lanes(along_x * 2 + along_z // 2)

    def cross_rows(part):
        if part != 2:
            return pl.ds(pl.multiple_of(tens * share, share), share)
        return pl.ds(pl.multiple_of(core * half, half), half)

    def cross_copy(part, mate, flip):
        at = cross_rows(part)
        return pltpu.make_async_remote_copy(
            src_ref=g.at[part, at, slice_of(mates[mate], part, flip)],
            dst_ref=mt.at[part, at, pl.ds((2 * mate - 2 + flip) * CHUNK, CHUNK)],
            send_sem=cross_send.at[part, mate, flip], recv_sem=cross_recv.at[part, mate, flip],
            device_id=(mate_id(mate), tens), device_id_type=MESH,
        )

    def twin_copy(part):
        piece = mt.at[part, cross_rows(part)]
        return pltpu.make_async_remote_copy(
            src_ref=piece, dst_ref=piece,
            send_sem=m_send.at[part, 2], recv_sem=m_recv.at[part, 2],
            device_id=(me, twin), device_id_type=MESH,
        )

    def cross_start(part):
        for mate in (1, 2, 3):
            for flip in range(2):
                cross_copy(part, mate, flip).start()

    def moved_begin(part):
        for mate in (1, 2, 3):
            for flip in range(2):
                cross_copy(part, mate, flip).wait_recv()
        if part != 2:
            begin(moved_hop, part)
        else:
            twin_copy(part).start()

    def multiply(part):
        weight_copy(part).wait()

        @pl.loop(0, columns)
        def _(column):
            at = lanes(column)
            weights = w_buf[part, :, :, at].reshape(g.shape[2], CHUNK)
            term = jnp.dot(g[part], weights, preferred_element_type=jnp.float32)
            if part == 0:
                weight_grad_ref[:, at] = term
            elif part < parts - 1:
                weight_grad_ref[:, at] += term
            else:
                qkv[:, at] = (weight_grad_ref[:, at] + term).astype(qkv.dtype)

    for part in range(parts):
        @pl.loop(1, peers)
        def _(step):
            move_copy(part, step).wait_recv()

        for slot in range(blocks):
            g[part, slot * BLK : (slot + 1) * BLK, lanes(tens)] = arrived[part][sources[slot]]
        begin(token_hop, part)
        if part > 0:
            last(token_hop, part - 1)
            complete(token_hop, part - 1)
            cross_start(part - 1)
            multiply(part - 1)
        onward(token_hop, part)
        if part == 2:
            moved_begin(0)
        if part == 3:
            onward(moved_hop, 0)
            moved_begin(1)
    last(token_hop, parts - 1)
    complete(token_hop, parts - 1)
    cross_start(parts - 1)
    multiply(parts - 1)

    factor = HD ** (-0.5)
    key_cols = pl.ds(GQ * HD, HD)
    value_cols = pl.ds((GQ + 1) * HD, HD)
    across = (((1,), (1,)), ((), ()))
    down_rows = (((0,), (0,)), ((), ()))

    def head(pair, which):
        cols = lanes(2 * pair + which, HD)
        for block in range(2):
            at = pl.ds(block * half, half)
            keys = pl.ds(0, (block + 1) * half)
            query = qkv[at, cols]
            key = qkv[keys, key_cols]
            value = qkv[keys, value_cols]
            grad_out = grad_ref[at, cols]
            scores = lax.dot_general(query, key, across, preferred_element_type=jnp.float32)
            scores = scores * factor + bias[at, keys].astype(jnp.float32)
            exponent = jnp.exp(scores - jnp.max(scores, axis=1, keepdims=True))
            prob = exponent * (1.0 / jnp.sum(exponent, axis=1, keepdims=True))
            prob_low = prob.astype(jnp.bfloat16)
            attn_ref[at, cols] = jnp.dot(
                prob_low, value, preferred_element_type=jnp.float32
            ).astype(attn_ref.dtype)
            grad_prob = lax.dot_general(grad_out, value, across, preferred_element_type=jnp.float32)
            row_dot = jnp.sum(prob * grad_prob, axis=1, keepdims=True)
            grad_score = (prob * (grad_prob - row_dot)).astype(jnp.bfloat16)
            grad_query = jnp.dot(grad_score, key, preferred_element_type=jnp.float32) * factor
            grads[0, pair, at, lanes(which, HD)] = grad_query.astype(grads.dtype)
            key_grad[keys, :] += lax.dot_general(
                grad_score, query, down_rows, preferred_element_type=jnp.float32
            )
            value_grad[keys, :] += lax.dot_general(
                prob_low, grad_out, down_rows, preferred_element_type=jnp.float32
            )

    def heads(pair):
        for which in range(2):
            head(pair, which)

    grad_routes = ((0, 1, 1, 0, rows), (0, 2, 2, 0, rows), (1, 2, 3, 0, half), (2, 1, 3, half, half))

    def grad_copy(pair, kind):
        source, mate, slot, first, count = grad_routes[kind]
        return pltpu.make_async_remote_copy(
            src_ref=grads.at[source, pair, pl.ds(first, count)],
            dst_ref=grads.at[slot, pair, pl.ds(first, count)],
            send_sem=grad_send.at[pair, kind], recv_sem=grad_recv.at[pair, kind],
            device_id=(mate_id(mate), tens), device_id_type=MESH,
        )

    def grad_begin(pair):
        grad_copy(pair, 0).start()
        grad_copy(pair, 1).start()

    def grad_onward(pair):
        grad_copy(pair, 0).wait_recv()
        grad_copy(pair, 2).start()
        grad_copy(pair, 1).wait_recv()
        grad_copy(pair, 3).start()

    def grad_complete(pair):
        grad_copy(pair, 2).wait_recv()
        grad_copy(pair, 3).wait_recv()

    heads(0)
    grad_begin(0)
    last(moved_hop, 0)
    onward(moved_hop, 1)
    moved_begin(3)
    moved_begin(2)
    heads(1)
    grad_begin(1)
    last(moved_hop, 1)
    onward(moved_hop, 3)
    heads(2)
    grad_begin(2)
    grad_onward(0)
    last(moved_hop, 3)
    heads(3)
    grad_begin(3)
    grads[0, GQ // 2, :, :HD] = (key_grad[...] * factor).astype(grads.dtype)
    grads[0, GQ // 2, :, HD:] = value_grad[...].astype(grads.dtype)
    grad_begin(4)

    for part in range(parts):
        for kind in range(8):
            token_hop(part, kind).wait_send()
        if part != 2:
            complete(moved_hop, part)
            for kind in range(8):
                moved_hop(part, kind).wait_send()
        else:
            twin_copy(part).wait()
        for mate in (1, 2, 3):
            for flip in range(2):
                cross_copy(part, mate, flip).wait_send()

        @pl.loop(1, peers)
        def _(step):
            move_copy(part, step).wait_send()

    def side_term(which, column):
        parity = (at_z + which // 2) % 2
        terms = []
        for side in range(2):
            total = None
            for mate in range(4):
                if mate == 0:
                    along_z = at_z if which < 2 else RING - 1 - at_z
                    along_x = at_x if which % 2 == 0 else RING - 1 - at_x
                    left = g[2 * parity + side, :, lanes(along_x * 2 + along_z // 2)]
                else:
                    left = mt[2 * parity + side, :, pl.ds((2 * mate - 2 + which % 2) * CHUNK, CHUNK)]
                term = lax.dot_general(
                    left, grads[mate, column], down_rows, preferred_element_type=jnp.float32
                )
                total = term if total is None else total + term
            terms.append(total)
        return terms

    def sum_copy(column, kind):
        source = (diag, diag, soon, soon, late, late)[kind].at[column, kind % 2]
        if kind < 2:
            dest = relay.at[column, kind]
        else:
            first = (half, 0, 0, half)[kind - 2]
            dest = summed.at[1 - kind % 2, column, pl.ds(first, half)]
        return pltpu.make_async_remote_copy(
            src_ref=source, dst_ref=dest,
            send_sem=sum_send.at[column, kind], recv_sem=sum_recv.at[column, kind],
            device_id=(adders[(1, 2, 2, 1, 2, 1)[kind]], tens), device_id_type=MESH,
        )

    def sum_onward(column):
        for side in range(2):
            sum_copy(column, side).wait_recv()
            both = late[column, side].astype(jnp.float32) + relay[column, side].astype(jnp.float32)
            late[column, side] = both.astype(late.dtype)
            sum_copy(column, 4 + side).start()

    def sum_complete(column):
        at = pl.ds(column * CHUNK, CHUNK)
        for kind in range(2, 6):
            sum_copy(column, kind).wait_recv()
        total = weight_grad_ref[:, at] + summed[0, column].astype(jnp.float32)
        weight_grad_ref[:, at] = total + summed[1, column].astype(jnp.float32)

    for column in range(columns):
        grad_complete(column)
        at = pl.ds(column * CHUNK, CHUNK)
        for which in (3, 2, 1, 0):
            low_half, high_half = side_term(which, column)
            if which == 3:
                diag[column, 0] = low_half.astype(diag.dtype)
                sum_copy(column, 0).start()
                diag[column, 1] = high_half.astype(diag.dtype)
                sum_copy(column, 1).start()
            elif which == 2:
                soon[column, 0] = high_half.astype(soon.dtype)
                sum_copy(column, 2).start()
                late[column, 0] = low_half.astype(late.dtype)
            elif which == 1:
                soon[column, 1] = low_half.astype(soon.dtype)
                sum_copy(column, 3).start()
                late[column, 1] = high_half.astype(late.dtype)
            else:
                weight_grad_ref[:half, at] = low_half
                weight_grad_ref[half:, at] = high_half
        if column + 1 < columns:
            grad_onward(column + 1)
        sum_onward(column)
        if column >= 2:
            sum_complete(column - 2)
    for column in (columns - 2, columns - 1):
        sum_complete(column)

    for column in range(columns):
        for kind in range(len(grad_routes)):
            grad_copy(column, kind).wait_send()
        for kind in range(6):
            sum_copy(column, kind).wait_send()


def local(tokens, block_target, doc_lengths, qkv_weight, out_grad):
    peers = lax.axis_size("dp")
    rows, width = tokens.shape
    blocks = rows // BLK
    parts = width // CHUNK
    depth, columns = qkv_weight.shape
    tensors = depth // width
    wide = depth // parts
    pairs = columns // CHUNK
    low = jnp.bfloat16
    dma = pltpu.SemaphoreType.DMA
    vmem = pl.BlockSpec(memory_space=pltpu.VMEM)
    smem = pl.BlockSpec(memory_space=pltpu.SMEM)
    return pl.pallas_call(
        step_kernel,
        out_shape=(
            jax.ShapeDtypeStruct(out_grad.shape, low),
            jax.ShapeDtypeStruct((rows, columns), jnp.float32),
        ),
        in_specs=[smem, smem, vmem, pl.BlockSpec(memory_space=pl.ANY), vmem],
        out_specs=(vmem, vmem),
        scratch_shapes=[
            pltpu.VMEM((8, 128), jnp.int32),
            pltpu.VMEM((peers, 8, 128), jnp.int32),
            pltpu.SMEM((peers, 8, 128), jnp.int32),
            pltpu.VMEM((parts, peers, BLK, CHUNK), low),
            *[pltpu.VMEM((peers, BLK, CHUNK), low) for _ in range(parts)],
            pltpu.VMEM((parts, rows, wide), low),
            pltpu.VMEM((parts, tensors, CHUNK, columns), low),
            pltpu.VMEM((rows, columns), low),
            pltpu.VMEM((parts, rows, 6 * CHUNK), low),
            pltpu.VMEM((4, pairs, rows, CHUNK), low),
            *[pltpu.VMEM((pairs, 2, rows // 2, CHUNK), low) for _ in range(4)],
            pltpu.VMEM((2, pairs, rows, CHUNK), low),
            pltpu.VMEM((rows, rows), low),
            pltpu.VMEM((rows, HD), jnp.float32),
            pltpu.VMEM((rows, HD), jnp.float32),
            dma((peers,)), dma((peers,)),
            dma((parts, peers)), dma((parts, peers)),
            dma((parts, 8)), dma((parts, 8)),
            dma((parts,)), dma,
            dma((parts, 4, 2)), dma((parts, 4, 2)),
            dma((parts, 8)), dma((parts, 8)),
            dma((pairs, 4)), dma((pairs, 4)),
            dma((pairs, 6)), dma((pairs, 6)),
        ],
        compiler_params=pltpu.CompilerParams(
            collective_id=0, has_side_effects=True, vmem_limit_bytes=64 * 2**20
        ),
    )(
        block_target,
        doc_lengths,
        tokens.reshape(blocks, BLK, width),
        qkv_weight.reshape(tensors, parts, CHUNK, columns),
        out_grad,
    )


def solution(mesh):
    placed = (P("dp", "tensor"), P("dp"), P("dp", None), P(None, "tensor"), P("dp", "tensor"))
    return jax.shard_map(
        local,
        mesh=mesh,
        in_specs=placed,
        out_specs=(P("dp", "tensor"), P("dp", "tensor")),
        check_vma=False,
    )
```

```python
import jax
import jax.numpy as jnp
from jax import lax
from jax.experimental import pallas as pl
from jax.experimental.pallas import tpu as pltpu
from jax.sharding import PartitionSpec as P

HD = 128
GQ = 8
BLK = 128
RING = 4
CHUNK = 256
MESH = pl.DeviceIdType.MESH


def peer_at(me, step):
    along_x = (me // RING + step // RING) % RING
    along_z = (me % RING + step % RING) % RING
    return along_x * RING + along_z


def step_kernel(
    target_ref, docs_ref, tok_ref, w_ref, grad_ref, attn_ref, weight_grad_ref,
    tag_out, tags, tags_smem, out_buf, arr0, arr1, arr2, arr3, g, w_buf, qkv,
    mt, grads, diag, soon, late, relay, summed, bias, key_grad, value_grad,
    tag_send, tag_recv, move_send, move_recv, y_send, y_recv, w_sem, smem_sem,
    cross_send, cross_recv, m_send, m_recv, grad_send, grad_recv, sum_send, sum_recv,
):
    arrived = (arr0, arr1, arr2, arr3)
    parts = len(arrived)
    blocks = tok_ref.shape[0]
    peers = tags.shape[0]
    rows = blocks * BLK
    half = rows // 2
    columns = weight_grad_ref.shape[1] // CHUNK
    me = lax.axis_index("dp")
    tens = lax.axis_index("tensor")
    at_x, at_z = me // RING, me % RING
    along_y, core = tens // 2, tens % 2
    up = ((along_y + 1) % RING) * 2 + core
    down = ((along_y + RING - 1) % RING) * 2 + core
    far = ((along_y + 2) % RING) * 2 + core
    twin = along_y * 2 + 1 - core
    near_x = at_x + 1 - 2 * (at_x % 2)
    near_z = at_z + 1 - 2 * (at_z % 2)
    mates = ((at_x, at_z), (near_x, at_z), (at_x, near_z), (near_x, near_z))
    adders = (
        me,
        (RING - 1 - at_x) * RING + at_z,
        at_x * RING + RING - 1 - at_z,
        (RING - 1 - at_x) * RING + RING - 1 - at_z,
    )

    def mate_id(mate):
        return mates[mate][0] * RING + mates[mate][1]

    def lanes(which, width=CHUNK):
        return pl.ds(pl.multiple_of(which * width, width), width)

    def weight_copy(part):
        return pltpu.make_async_copy(w_ref.at[:, part], w_buf.at[part], w_sem.at[part])

    for part in range(parts):
        weight_copy(part).start()

    row_of = lax.broadcasted_iota(jnp.int32, tag_out.shape, 0)
    tile = jnp.zeros(tag_out.shape, jnp.int32)
    for slot in range(blocks):
        tile = jnp.where(row_of == slot, target_ref[slot], tile)
    tag_out[...] = tile

    barrier = pltpu.get_barrier_semaphore()

    @pl.loop(1, peers)
    def _(step):
        pl.semaphore_signal(barrier, inc=1, device_id=(peer_at(me, step), tens), device_id_type=MESH)

    for other in (up, down, twin):
        pl.semaphore_signal(barrier, inc=1, device_id=(me, other), device_id_type=MESH)

    def block_for(peer):
        picked = jnp.int32(0)
        for slot in range(blocks):
            picked = jnp.where(target_ref[slot] // blocks == peer, slot, picked)
        return picked

    def pack(part):
        @pl.loop(0, peers)
        def _(peer):
            out_buf[part, peer] = tok_ref[block_for(peer), :, part * CHUNK : (part + 1) * CHUNK]

    def tag_copy(step):
        return pltpu.make_async_remote_copy(
            src_ref=tag_out, dst_ref=tags.at[me],
            send_sem=tag_send.at[step], recv_sem=tag_recv.at[step],
            device_id=(peer_at(me, step), tens), device_id_type=MESH,
        )

    def move_copy(part, step):
        peer = peer_at(me, step)
        return pltpu.make_async_remote_copy(
            src_ref=out_buf.at[part, peer], dst_ref=arrived[part].at[me],
            send_sem=move_send.at[part, step], recv_sem=move_recv.at[part, step],
            device_id=(peer, tens), device_id_type=MESH,
        )

    def send_part(part):
        @pl.loop(1, peers)
        def _(step):
            move_copy(part, step).start()

        arrived[part][me] = out_buf[part, me]

    pack(0)
    pl.semaphore_wait(barrier, peers - 1 + 3)

    @pl.loop(1, peers)
    def _(step):
        tag_copy(step).start()

    send_part(0)
    for part in range(1, parts):
        pack(part)
        send_part(part)
    tags[me] = tag_out[...]

    query_at = lax.broadcasted_iota(jnp.int32, bias.shape, 0)
    key_at = lax.broadcasted_iota(jnp.int32, bias.shape, 1)
    allowed = key_at <= query_at
    doc_end = jnp.int32(0)
    for doc in range(docs_ref.shape[1]):
        doc_end = doc_end + docs_ref[0, doc]
        allowed = allowed & ((query_at >= doc_end) == (key_at >= doc_end))
    bias[...] = jnp.where(allowed, 0.0, -jnp.inf).astype(bias.dtype)
    key_grad[...] = jnp.zeros_like(key_grad)
    value_grad[...] = jnp.zeros_like(value_grad)

    @pl.loop(1, peers)
    def _(step):
        tag_copy(step).wait()

    to_smem = pltpu.make_async_copy(tags, tags_smem, smem_sem)
    to_smem.start()
    to_smem.wait()

    def source_of(slot):
        def look(peer, found):
            for entry in range(blocks):
                found = jnp.where(tags_smem[peer, entry, 0] == me * blocks + slot, peer, found)
            return found

        return lax.fori_loop(0, peers, look, jnp.int32(0))

    sources = [source_of(slot) for slot in range(blocks)]

    def ring_routes(count):
        return (
            (tens, up, 0, count),
            (tens, down, 0, count),
            (tens, twin, 0, count),
            (down, up, 0, count // 2),
            (down, twin, 0, count),
            (up, down, count // 2, count // 2),
            (up, twin, 0, count),
            (far, twin, 0, count),
        )

    share = rows // 8
    token_routes = ring_routes(rows)
    moved_routes = ring_routes(share)

    def token_hop(part, kind):
        owner, dest, first, count = token_routes[kind]
        piece = g.at[part, pl.ds(first, count), lanes(owner)]
        return pltpu.make_async_remote_copy(
            src_ref=piece, dst_ref=piece,
            send_sem=y_send.at[part, kind], recv_sem=y_recv.at[part, kind],
            device_id=(me, dest), device_id_type=MESH,
        )

    def moved_hop(part, kind):
        owner, dest, first, count = moved_routes[kind]
        at = pl.ds(pl.multiple_of(owner * share + first, 16), count)
        piece = mt.at[part, at, pl.ds(0, 6 * CHUNK)]
        return pltpu.make_async_remote_copy(
            src_ref=piece, dst_ref=piece,
            send_sem=m_send.at[part, kind], recv_sem=m_recv.at[part, kind],
            device_id=(me, dest), device_id_type=MESH,
        )

    def begin(hop, part):
        for kind in (0, 1, 2):
            hop(part, kind).start()

    def onward(hop, part):
        hop(part, 0).wait_recv()
        hop(part, 3).start()
        hop(part, 4).start()
        hop(part, 1).wait_recv()
        hop(part, 5).start()
        hop(part, 6).start()

    def last(hop, part):
        hop(part, 3).wait_recv()
        hop(part, 5).wait_recv()
        hop(part, 7).start()

    def complete(hop, part):
        for kind in (2, 4, 6, 7):
            hop(part, kind).wait_recv()

    def slice_of(device, part, flip):
        along_x, along_z = device
        along_x = RING - 1 - along_x if flip else along_x
        along_z = along_z + (RING - 1 - 2 * along_z) * ((along_z + part // 2) % 2)
        return lanes(along_x * 2 + along_z // 2)

    def cross_rows(part):
        if part != 2:
            return pl.ds(pl.multiple_of(tens * share, share), share)
        return pl.ds(pl.multiple_of(core * half, half), half)

    def cross_copy(part, mate, flip):
        at = cross_rows(part)
        return pltpu.make_async_remote_copy(
            src_ref=g.at[part, at, slice_of(mates[mate], part, flip)],
            dst_ref=mt.at[part, at, pl.ds((2 * mate - 2 + flip) * CHUNK, CHUNK)],
            send_sem=cross_send.at[part, mate, flip], recv_sem=cross_recv.at[part, mate, flip],
            device_id=(mate_id(mate), tens), device_id_type=MESH,
        )

    def twin_copy(part):
        piece = mt.at[part, cross_rows(part)]
        return pltpu.make_async_remote_copy(
            src_ref=piece, dst_ref=piece,
            send_sem=m_send.at[part, 2], recv_sem=m_recv.at[part, 2],
            device_id=(me, twin), device_id_type=MESH,
        )

    def cross_start(part):
        for mate in (1, 2, 3):
            for flip in range(2):
                cross_copy(part, mate, flip).start()

    def moved_begin(part):
        for mate in (1, 2, 3):
            for flip in range(2):
                cross_copy(part, mate, flip).wait_recv()
        if part != 2:
            begin(moved_hop, part)
        else:
            twin_copy(part).start()

    def multiply(part):
        weight_copy(part).wait()

        @pl.loop(0, columns)
        def _(column):
            at = lanes(column)
            weights = w_buf[part, :, :, at].reshape(g.shape[2], CHUNK)
            term = jnp.dot(g[part], weights, preferred_element_type=jnp.float32)
            if part == 0:
                weight_grad_ref[:, at] = term
            elif part < parts - 1:
                weight_grad_ref[:, at] += term
            else:
                qkv[:, at] = (weight_grad_ref[:, at] + term).astype(qkv.dtype)

    for part in range(parts):
        @pl.loop(1, peers)
        def _(step):
            move_copy(part, step).wait_recv()

        for slot in range(blocks):
            g[part, slot * BLK : (slot + 1) * BLK, lanes(tens)] = arrived[part][sources[slot]]
        begin(token_hop, part)
        if part > 0:
            last(token_hop, part - 1)
            complete(token_hop, part - 1)
            cross_start(part - 1)
            multiply(part - 1)
        onward(token_hop, part)
        if part == 2:
            moved_begin(0)
        if part == 3:
            onward(moved_hop, 0)
            moved_begin(1)
    last(token_hop, parts - 1)
    complete(token_hop, parts - 1)
    cross_start(parts - 1)
    multiply(parts - 1)

    factor = HD ** (-0.5)
    key_cols = pl.ds(GQ * HD, HD)
    value_cols = pl.ds((GQ + 1) * HD, HD)
    across = (((1,), (1,)), ((), ()))
    down_rows = (((0,), (0,)), ((), ()))

    def head(pair, which):
        cols = lanes(2 * pair + which, HD)
        for block in range(2):
            at = pl.ds(block * half, half)
            keys = pl.ds(0, (block + 1) * half)
            query = qkv[at, cols]
            key = qkv[keys, key_cols]
            value = qkv[keys, value_cols]
            grad_out = grad_ref[at, cols]
            scores = lax.dot_general(query, key, across, preferred_element_type=jnp.float32)
            scores = scores * factor + bias[at, keys].astype(jnp.float32)
            exponent = jnp.exp(scores - jnp.max(scores, axis=1, keepdims=True))
            prob = exponent * (1.0 / jnp.sum(exponent, axis=1, keepdims=True))
            prob_low = prob.astype(jnp.bfloat16)
            attn_ref[at, cols] = jnp.dot(
                prob_low, value, preferred_element_type=jnp.float32
            ).astype(attn_ref.dtype)
            grad_prob = lax.dot_general(grad_out, value, across, preferred_element_type=jnp.float32)
            row_dot = jnp.sum(prob * grad_prob, axis=1, keepdims=True)
            grad_score = (prob * (grad_prob - row_dot)).astype(jnp.bfloat16)
            grad_query = jnp.dot(grad_score, key, preferred_element_type=jnp.float32) * factor
            grads[0, pair, at, lanes(which, HD)] = grad_query.astype(grads.dtype)
            key_grad[keys, :] += lax.dot_general(
                grad_score, query, down_rows, preferred_element_type=jnp.float32
            )
            value_grad[keys, :] += lax.dot_general(
                prob_low, grad_out, down_rows, preferred_element_type=jnp.float32
            )

    def heads(pair):
        for which in range(2):
            head(pair, which)

    grad_routes = ((0, 1, 1, 0, rows), (0, 2, 2, 0, rows), (1, 2, 3, 0, half), (2, 1, 3, half, half))

    def grad_copy(pair, kind):
        source, mate, slot, first, count = grad_routes[kind]
        return pltpu.make_async_remote_copy(
            src_ref=grads.at[source, pair, pl.ds(first, count)],
            dst_ref=grads.at[slot, pair, pl.ds(first, count)],
            send_sem=grad_send.at[pair, kind], recv_sem=grad_recv.at[pair, kind],
            device_id=(mate_id(mate), tens), device_id_type=MESH,
        )

    def grad_begin(pair):
        grad_copy(pair, 0).start()
        grad_copy(pair, 1).start()

    def grad_onward(pair):
        grad_copy(pair, 0).wait_recv()
        grad_copy(pair, 2).start()
        grad_copy(pair, 1).wait_recv()
        grad_copy(pair, 3).start()

    def grad_complete(pair):
        grad_copy(pair, 2).wait_recv()
        grad_copy(pair, 3).wait_recv()

    heads(0)
    grad_begin(0)
    last(moved_hop, 0)
    onward(moved_hop, 1)
    moved_begin(3)
    moved_begin(2)
    heads(1)
    grad_begin(1)
    last(moved_hop, 1)
    onward(moved_hop, 3)
    heads(2)
    grad_onward(0)
    grad_begin(2)
    last(moved_hop, 3)
    heads(3)
    grad_onward(1)
    grad_begin(3)
    grads[0, GQ // 2, :, :HD] = (key_grad[...] * factor).astype(grads.dtype)
    grads[0, GQ // 2, :, HD:] = value_grad[...].astype(grads.dtype)

    for part in range(parts):
        for kind in range(8):
            token_hop(part, kind).wait_send()
        if part != 2:
            complete(moved_hop, part)
            for kind in range(8):
                moved_hop(part, kind).wait_send()
        else:
            twin_copy(part).wait()
        for mate in (1, 2, 3):
            for flip in range(2):
                cross_copy(part, mate, flip).wait_send()

        @pl.loop(1, peers)
        def _(step):
            move_copy(part, step).wait_send()

    def side_term(which, column):
        parity = (at_z + which // 2) % 2
        terms = []
        for side in range(2):
            total = None
            for mate in range(4):
                if mate == 0:
                    along_z = at_z if which < 2 else RING - 1 - at_z
                    along_x = at_x if which % 2 == 0 else RING - 1 - at_x
                    left = g[2 * parity + side, :, lanes(along_x * 2 + along_z // 2)]
                else:
                    left = mt[2 * parity + side, :, pl.ds((2 * mate - 2 + which % 2) * CHUNK, CHUNK)]
                term = lax.dot_general(
                    left, grads[mate, column], down_rows, preferred_element_type=jnp.float32
                )
                total = term if total is None else total + term
            terms.append(total)
        return terms

    def sum_copy(column, kind):
        source = (diag, diag, soon, soon, late, late)[kind].at[column, kind % 2]
        if kind < 2:
            dest = relay.at[column, kind]
        else:
            first = (half, 0, 0, half)[kind - 2]
            dest = summed.at[1 - kind % 2, column, pl.ds(first, half)]
        return pltpu.make_async_remote_copy(
            src_ref=source, dst_ref=dest,
            send_sem=sum_send.at[column, kind], recv_sem=sum_recv.at[column, kind],
            device_id=(adders[(1, 2, 2, 1, 2, 1)[kind]], tens), device_id_type=MESH,
        )

    def sum_onward(column):
        for side in range(2):
            sum_copy(column, side).wait_recv()
            both = late[column, side].astype(jnp.float32) + relay[column, side].astype(jnp.float32)
            late[column, side] = both.astype(late.dtype)
            sum_copy(column, 4 + side).start()

    def sum_complete(column):
        at = pl.ds(column * CHUNK, CHUNK)
        for kind in range(2, 6):
            sum_copy(column, kind).wait_recv()
        total = weight_grad_ref[:, at] + summed[0, column].astype(jnp.float32)
        weight_grad_ref[:, at] = total + summed[1, column].astype(jnp.float32)

    for column in range(columns):
        grad_complete(column)
        at = pl.ds(column * CHUNK, CHUNK)
        for which in (3, 2, 1, 0):
            low_half, high_half = side_term(which, column)
            if which == 3:
                diag[column, 0] = low_half.astype(diag.dtype)
                sum_copy(column, 0).start()
                diag[column, 1] = high_half.astype(diag.dtype)
                sum_copy(column, 1).start()
            elif which == 2:
                soon[column, 0] = high_half.astype(soon.dtype)
                sum_copy(column, 2).start()
                late[column, 0] = low_half.astype(late.dtype)
            elif which == 1:
                soon[column, 1] = low_half.astype(soon.dtype)
                sum_copy(column, 3).start()
                late[column, 1] = high_half.astype(late.dtype)
            else:
                weight_grad_ref[:half, at] = low_half
                weight_grad_ref[half:, at] = high_half
        if column + 2 < columns:
            grad_onward(column + 2)
        if column == 0:
            grad_begin(columns - 1)
        sum_onward(column)
        if column >= 2:
            sum_complete(column - 2)
    for column in (columns - 2, columns - 1):
        sum_complete(column)

    for column in range(columns):
        for kind in range(len(grad_routes)):
            grad_copy(column, kind).wait_send()
        for kind in range(6):
            sum_copy(column, kind).wait_send()


def local(tokens, block_target, doc_lengths, qkv_weight, out_grad):
    peers = lax.axis_size("dp")
    rows, width = tokens.shape
    blocks = rows // BLK
    parts = width // CHUNK
    depth, columns = qkv_weight.shape
    tensors = depth // width
    wide = depth // parts
    pairs = columns // CHUNK
    low = jnp.bfloat16
    dma = pltpu.SemaphoreType.DMA
    vmem = pl.BlockSpec(memory_space=pltpu.VMEM)
    smem = pl.BlockSpec(memory_space=pltpu.SMEM)
    return pl.pallas_call(
        step_kernel,
        out_shape=(
            jax.ShapeDtypeStruct(out_grad.shape, low),
            jax.ShapeDtypeStruct((rows, columns), jnp.float32),
        ),
        in_specs=[smem, smem, vmem, pl.BlockSpec(memory_space=pl.ANY), vmem],
        out_specs=(vmem, vmem),
        scratch_shapes=[
            pltpu.VMEM((8, 128), jnp.int32),
            pltpu.VMEM((peers, 8, 128), jnp.int32),
            pltpu.SMEM((peers, 8, 128), jnp.int32),
            pltpu.VMEM((parts, peers, BLK, CHUNK), low),
            *[pltpu.VMEM((peers, BLK, CHUNK), low) for _ in range(parts)],
            pltpu.VMEM((parts, rows, wide), low),
            pltpu.VMEM((parts, tensors, CHUNK, columns), low),
            pltpu.VMEM((rows, columns), low),
            pltpu.VMEM((parts, rows, 6 * CHUNK), low),
            pltpu.VMEM((4, pairs, rows, CHUNK), low),
            *[pltpu.VMEM((pairs, 2, rows // 2, CHUNK), low) for _ in range(4)],
            pltpu.VMEM((2, pairs, rows, CHUNK), low),
            pltpu.VMEM((rows, rows), low),
            pltpu.VMEM((rows, HD), jnp.float32),
            pltpu.VMEM((rows, HD), jnp.float32),
            dma((peers,)), dma((peers,)),
            dma((parts, peers)), dma((parts, peers)),
            dma((parts, 8)), dma((parts, 8)),
            dma((parts,)), dma,
            dma((parts, 4, 2)), dma((parts, 4, 2)),
            dma((parts, 8)), dma((parts, 8)),
            dma((pairs, 4)), dma((pairs, 4)),
            dma((pairs, 6)), dma((pairs, 6)),
        ],
        compiler_params=pltpu.CompilerParams(
            collective_id=0, has_side_effects=True, vmem_limit_bytes=64 * 2**20
        ),
    )(
        block_target,
        doc_lengths,
        tokens.reshape(blocks, BLK, width),
        qkv_weight.reshape(tensors, parts, CHUNK, columns),
        out_grad,
    )


def solution(mesh):
    placed = (P("dp", "tensor"), P("dp"), P("dp", None), P(None, "tensor"), P("dp", "tensor"))
    return jax.shard_map(
        local,
        mesh=mesh,
        in_specs=placed,
        out_specs=(P("dp", "tensor"), P("dp", "tensor")),
        check_vma=False,
    )
```
